512 devices in a mesh: dp: 16 (over y, z_hi, core), frame: 32 (over z_lo, x).
Axes of the slice: x: 4, y: 4, z: 16 (z_hi: 2, z_lo: 8; z = z_hi * 8 + z_lo), core: 2. Of those that a mesh axis runs over, the one named last changes fastest.
Arguments:
- video: bfloat16 [16, 32, 24, 64, 320], P('dp', 'frame'), may hold values from -18 to 18
- frame_emb: float32 [16, 32, 320], P('dp', 'frame'), may hold values from -12 to 12
- norm1_gain: float32 [320], replicated, may hold values from 0.1 to 1.9
- norm1_shift: float32 [320], replicated, may hold values from -3 to 3
- norm2_gain: float32 [320], replicated, may hold values from 0.1 to 1.9
- norm2_shift: float32 [320], replicated, may hold values from -3 to 3
- spatial_weight: bfloat16 [3, 960, 320], P(None, 'frame', 'dp'), may hold values from -0.109375 to 0.109375
- temporal_weight: bfloat16 [3, 320, 320], P(None, 'frame', 'dp'), may hold values from -0.1875 to 0.1875
- temporal_bias: float32 [320], replicated, may hold values from -3 to 3
Outputs:
- block_out: bfloat16 [16, 32, 24, 64, 320], P('dp', 'frame')
The draws below stay inside these ranges and needn't reach their ends.
All inputs are finite; a program needn't handle non-finite values.
Results may differ from the reference program's by a relative error of at most 0.0055.
Values may be sent and summed in bfloat16 or wider, within the bound.
No kernel may reach another device: no remote copies, remote signals or barrier semaphores. Data moves between devices by JAX's collectives and lax.ppermute only.
A program may use at most 64 MiB of HBM per device.

```python
import math
import jax
import jax.numpy as jnp
from jax import lax

C = 320
GROUPS = 32
H_ROWS = 24
W_COLS = 64
FRAMES = 32
VIDEOS = 16


def draw_video(key, part):
    key = jax.random.fold_in(key, 11)
    noise_key, channel_key, pixel_key = jax.random.split(key, 3)
    full_shape = (VIDEOS, FRAMES, H_ROWS, W_COLS, C)
    channel_scale = jnp.exp(jax.random.uniform(channel_key, (C,), jnp.float32, math.log(0.3), math.log(3.0)))
    pixel_scale = jnp.exp(jax.random.uniform(pixel_key, (VIDEOS, FRAMES, H_ROWS, W_COLS, 1), jnp.float32, math.log(0.5), math.log(2.0)))
    base_values = jnp.clip(jax.random.normal(noise_key, full_shape, jnp.float32), -3.0, 3.0)
    return (base_values * channel_scale * pixel_scale).astype(jnp.bfloat16)


def draw_frame_emb(key, part):
    key = jax.random.fold_in(key, 23)
    full_shape = (VIDEOS, FRAMES, C)
    position = jnp.arange(FRAMES, dtype=jnp.float32) / (FRAMES - 1)
    frame_ramp = 0.4 * jnp.exp(position * math.log(10.0))
    base_values = jnp.clip(jax.random.normal(key, full_shape, jnp.float32), -3.0, 3.0)
    return base_values * frame_ramp[None, :, None]


def shard_levels(rng, shape, cuts, low, largest):
    def one(axis_at, parts):
        heights = jax.random.uniform(jax.random.fold_in(jax.random.fold_in(rng, 6), axis_at), (parts,), jnp.float32, low / len(cuts), largest / len(cuts))
        return jnp.repeat(jnp.exp(heights), shape[axis_at] // parts).reshape((-1,) + (1,) * (len(shape) - axis_at - 1))

    factor_of = one(*cuts[0])
    for cut in cuts[1:]:
        factor_of = factor_of * one(*cut)
    return factor_of


def scatter_about(own_key, dims, width, most, pieces=(), kind=jnp.bfloat16):
    drawn = jax.random.normal(own_key, dims, jnp.float32) * width
    if len(pieces) > 0:
        drawn = shard_levels(own_key, dims, pieces, -0.22, 0.18) * drawn
    return jnp.clip(drawn, min=-most, max=most).astype(kind)


def setup_inputs(seed: int = 0) -> dict:
    seeds = jax.random.split(jax.random.key(seed), 10)
    return {
        "video": draw_video(jax.random.fold_in(seeds[9], 71), 0),
        "frame_emb": draw_frame_emb(jax.random.fold_in(seeds[9], 71), 0),
        "norm1_gain": jnp.clip(1.0 + 0.18 * jax.random.normal(seeds[2], (C,), jnp.float32), 0.1, 1.9),
        "norm1_shift": scatter_about(seeds[3], (C,), 0.5, 3.0, (), jnp.float32),
        "norm2_gain": jnp.clip(1.0 + 0.18 * jax.random.normal(seeds[4], (C,), jnp.float32), 0.1, 1.9),
        "norm2_shift": scatter_about(seeds[5], (C,), 0.5, 3.0, (), jnp.float32),
        "spatial_weight": scatter_about(seeds[6], (3, 3 * C, C), (9 * C) ** -0.5, 0.109375, ((1, 32), (2, 16))),
        "temporal_weight": scatter_about(seeds[7], (3, C, C), (3 * C) ** -0.5, 0.1875, ((1, 32), (2, 16))),
        "temporal_bias": scatter_about(seeds[8], (C,), 0.5, 3.0, (), jnp.float32),
    }


epsilon = 1e-05

def spatial_conv(activated, spatial_weight):
    frames, height, breadth, channels = activated.shape
    padded = jnp.pad(activated, ((0, 0), (1, 1), (1, 1), (0, 0)))
    summed = jnp.zeros((frames * height * breadth, channels), jnp.float32)
    for row_tap in range(3):
        columns = jnp.concatenate([padded[:, row_tap:row_tap + height, col_tap:col_tap + breadth, :] for col_tap in range(3)], axis=-1)
        summed = summed + jnp.dot(columns.reshape(-1, 3 * channels), spatial_weight[row_tap], preferred_element_type=jnp.float32)
    return summed

def reference(video, frame_emb, norm1_gain, norm1_shift, norm2_gain, norm2_shift, spatial_weight, temporal_weight, temporal_bias):

    def one_video(inputs_pair):
        clip_values, embedding = inputs_pair
        frames, height, breadth, channels = clip_values.shape
        group_width = channels // GROUPS
        flattened = clip_values.astype(jnp.float32).reshape(frames, height * breadth, GROUPS, group_width)
        average = lax.optimization_barrier(jnp.mean(flattened, axis=(1, 3)))
        variance = lax.optimization_barrier(jnp.mean(flattened * flattened, axis=(1, 3))) - average * average
        normed = (flattened - average[:, None, :, None]) * lax.rsqrt(variance + epsilon)[:, None, :, None]
        normed = normed.reshape(frames, height, breadth, channels) * norm1_gain + norm1_shift
        activated = jax.nn.silu(normed).astype(jnp.bfloat16)
        summed = spatial_conv(activated, spatial_weight).reshape(frames, height * breadth, channels)
        hidden = (summed + embedding[:, None, :]).astype(jnp.bfloat16)
        grouped = hidden.astype(jnp.float32).reshape(-1, GROUPS, group_width)
        average2 = lax.optimization_barrier(jnp.mean(grouped, axis=(0, 2)))
        variance2 = lax.optimization_barrier(jnp.mean(grouped * grouped, axis=(0, 2))) - average2 * average2
        normed2 = (grouped - average2[None, :, None]) * lax.rsqrt(variance2 + epsilon)[None, :, None]
        normed2 = normed2.reshape(frames, height * breadth, channels) * norm2_gain + norm2_shift
        mixed = jax.nn.silu(normed2).astype(jnp.bfloat16)
        padded = jnp.pad(mixed, ((1, 1), (0, 0), (0, 0)))
        temporal_sum = jnp.zeros((frames * height * breadth, channels), jnp.float32)
        for offset in range(3):
            temporal_sum = temporal_sum + jnp.dot(padded[offset:offset + frames].reshape(-1, channels), temporal_weight[offset], preferred_element_type=jnp.float32)
        temporal_out = (temporal_sum + temporal_bias).astype(jnp.bfloat16)
        result = hidden.reshape(-1, channels).astype(jnp.float32) + temporal_out.astype(jnp.float32)
        return result.astype(jnp.bfloat16).reshape(frames, height, breadth, channels)
    return lax.map(one_video, (video, frame_emb))
```

```python
import functools

import jax
import jax.numpy as jnp
import numpy as np
from jax import lax
from jax.experimental import pallas as pl
from jax.experimental.pallas import tpu as pltpu
from jax.sharding import Mesh, PartitionSpec as P

GROUPS = 32
C = 320
CELLS = 1536
COLS = 64
EPS = 1e-5
BF = jnp.bfloat16
F32 = jnp.float32
KPAD = 1024
CPAD = 384
HALF = 192
VMEM = 48 * 1024 * 1024


def _consts():
    act_perm = np.zeros((3, C, KPAD), np.float32)
    for f in range(32):
        zl, x = divmod(f, 4)
        for kk in range(30):
            b, i = divmod(30 * f + kk, C)
            act_perm[b, i, 256 * x + 30 * zl + kk] = 1
    piece_perm = np.zeros((8, 128, KPAD), np.float32)
    for zl in range(8):
        for a in range(3):
            for kk in range(30):
                piece_perm[zl, 30 * a + kk, 256 * a + 30 * zl + kk] = 1
            for kk in range(10):
                piece_perm[zl, 90 + 10 * a + kk, 768 + 80 * a + 10 * zl + kk] = 1
    chan = np.zeros(C, np.int64)
    for i in range(C):
        d, j = divmod(i, 20)
        y, zh, core = d // 4, (d // 2) % 2, d % 2
        chan[i] = HALF * core + 48 * y + 24 * zh + j
    order = np.zeros((C, CPAD), np.float32)
    order[np.arange(C), chan] = 1
    temp_perm = np.zeros((KPAD, 3 * CPAD), np.float32)
    for x in range(4):
        for t in range(3):
            for zl in range(8):
                for kk in range(10):
                    i = 40 * zl + 10 * x + kk
                    temp_perm[256 * x + 80 * t + 10 * zl + kk, CPAD * t + chan[i]] = 1
    same1 = np.kron(np.eye(GROUPS), np.ones((10, 10))).astype(np.float32)
    same2 = order.T @ same1 @ order
    pack_s = np.zeros((3, 30, 128), np.float32)
    pack_t = np.zeros((3, 10, 128), np.float32)
    for a in range(3):
        pack_s[a, np.arange(30), 30 * a + np.arange(30)] = 1
        pack_t[a, np.arange(10), 90 + 10 * a + np.arange(10)] = 1
    return act_perm, piece_perm, order, temp_perm, same1, same2, pack_s, pack_t


ACT_PERM, PIECE_PERM, ORDER, TEMP_PERM, SAME1, SAME2, PACK_S, PACK_T = _consts()


def call(kernel, out_shape, flops=0, scratch=(), smem=0, n=0):
    specs = [pl.BlockSpec(memory_space=pltpu.SMEM)] * smem + [pl.BlockSpec(memory_space=pltpu.VMEM)] * n
    return pl.pallas_call(
        kernel,
        out_shape=out_shape,
        in_specs=specs,
        out_specs=jax.tree.map(lambda _: pl.BlockSpec(memory_space=pltpu.VMEM), out_shape),
        scratch_shapes=list(scratch),
        compiler_params=pltpu.CompilerParams(vmem_limit_bytes=VMEM),
        cost_estimate=pl.CostEstimate(flops=flops, bytes_accessed=4_000_000, transcendentals=0),
    )


def exact(a, b):
    return jnp.dot(a, b, precision=lax.Precision.HIGHEST, preferred_element_type=F32)


def nt(a, b):
    return lax.dot_general(a, b, (((1,), (1,)), ((), ())), preferred_element_type=F32)


def silu(v):
    half = 0.5 * v
    return half + half * jnp.tanh(half)


def pack_kernel(sw, tw, ps, pt, out):
    total = jnp.zeros((20, 128), F32)
    for a in range(3):
        total += lax.dot_general(sw[a], ps[a], (((0,), (0,)), ((), ())), preferred_element_type=F32)
        total += lax.dot_general(tw[a], pt[a], (((0,), (0,)), ((), ())), preferred_element_type=F32)
    piece = jnp.concatenate([total, jnp.zeros((4, 128), F32)], axis=0).astype(BF)
    for n in range(16):
        out[n] = piece


def line_kernel(pieces, perm, out):
    total = jnp.zeros((48, KPAD), F32)
    for zl in range(8):
        both = jnp.concatenate([pieces[zl].astype(F32), pieces[8 + zl].astype(F32)], axis=0)
        total += jnp.dot(both.astype(BF), perm[zl], preferred_element_type=F32)
    block = total.astype(BF)
    for n in range(16):
        out[n] = block


def act_kernel(video, gain, shift, same, perm, out):
    chunk = 256

    def sums(i, carry):
        s, q = carry
        v = video[pl.ds(pl.multiple_of(i * chunk, chunk), chunk), :].astype(F32).reshape(chunk // 8, 8, C)
        return s + jnp.sum(v, axis=0), q + jnp.sum(v * v, axis=0)

    zero = jnp.zeros((8, C), F32)
    s, q = lax.fori_loop(0, CELLS // chunk, sums, (zero, zero))
    count = CELLS * C // GROUPS
    mean = jnp.sum(exact(s, same[...]), axis=0, keepdims=True) / count
    square = jnp.sum(exact(q, same[...]), axis=0, keepdims=True) / count
    scale = lax.rsqrt(square - mean * mean + EPS) * gain[...]
    offset = shift[...] - mean * scale
    column = lax.rem(lax.broadcasted_iota(jnp.int32, (chunk, C), 0), COLS)
    out[pl.ds(0, COLS), :] = jnp.zeros((COLS, KPAD), BF)
    out[pl.ds(CELLS + COLS, COLS), :] = jnp.zeros((COLS, KPAD), BF)

    def rows(i, carry):
        v = video[pl.ds(pl.multiple_of(i * chunk, chunk), chunk), :].astype(F32)
        v = silu(v * scale + offset).astype(BF).astype(F32)
        before = jnp.where(column == 0, 0.0, pltpu.roll(v, 1, 0)).astype(BF)
        after = jnp.where(column == COLS - 1, 0.0, pltpu.roll(v, chunk - 1, 0)).astype(BF)
        total = jnp.dot(before, perm[0], preferred_element_type=F32)
        total += jnp.dot(v.astype(BF), perm[1], preferred_element_type=F32)
        total += jnp.dot(after, perm[2], preferred_element_type=F32)
        out[pl.ds(pl.multiple_of(i * chunk + COLS, COLS), chunk), :] = total.astype(BF)
        return carry

    lax.fori_loop(0, CELLS // chunk, rows, 0)


def place_weights(core, own, other, w):
    mine = core * HALF
    theirs = HALF - mine
    for y in range(4):
        for x in range(4):
            for a in range(3):
                lanes = pl.ds(256 * x, 256)
                w[a, pl.ds(pl.multiple_of(mine + 48 * y, 16), 48), lanes] = own[4 * y + x, :, 256 * a : 256 * a + 256]
                w[a, pl.ds(pl.multiple_of(theirs + 48 * y, 16), 48), lanes] = other[4 * y + x, :, 256 * a : 256 * a + 256]


def convolve(cols, w, emb, hidden, stats):
    chunk = 512

    def rows(i, carry):
        s, q = carry
        total = jnp.zeros((chunk, CPAD), F32)
        for a in range(3):
            part = cols[pl.ds(pl.multiple_of(i * chunk + COLS * a, COLS), chunk), :]
            total += nt(part, w[a])
        h = (total + emb).astype(BF)
        hidden[pl.ds(pl.multiple_of(i * chunk, chunk), chunk), :] = h
        if not stats:
            return carry
        h = h.astype(F32).reshape(chunk // 8, 8, CPAD)
        return s + jnp.sum(h, axis=0), q + jnp.sum(h * h, axis=0)

    zero = jnp.zeros((8, CPAD), F32)
    return lax.fori_loop(0, CELLS // chunk, rows, (zero, zero))


def own_kernel(core, cols, own, other, emb, hidden, stats, w):
    place_weights(core[0], own, other, w)
    s, q = convolve(cols, w, emb[...], hidden, True)
    s = jnp.sum(s, axis=0, keepdims=True)
    q = jnp.sum(q, axis=0, keepdims=True)
    rows = [s[:, :128], s[:, 128:256], s[:, 256:], q[:, :128], q[:, 128:256], q[:, 256:], jnp.zeros((2, 128), F32)]
    block = jnp.concatenate(rows, axis=0)
    for n in range(32):
        stats[n] = block


def near_kernel(core, before, after, own, other, emb0, emb2, hidden0, hidden2, w):
    place_weights(core[0], own, other, w)
    convolve(before, w, emb0[...], hidden0, False)
    convolve(after, w, emb2[...], hidden2, False)


def temporal_kernel(core, keep, own, other, perm, order, out, w):
    mine = core[0] * HALF
    theirs = HALF - mine
    for y in range(4):
        for x in range(4):
            lanes = pl.ds(256 * x, 256)
            w[pl.ds(pl.multiple_of(mine + 48 * y, 16), 48), lanes] = own[4 * y + x, :, 768:]
            w[pl.ds(pl.multiple_of(theirs + 48 * y, 16), 48), lanes] = other[4 * y + x, :, 768:]
    for t in range(3):
        part = jnp.dot(w[...], perm[:, CPAD * t : CPAD * t + CPAD], preferred_element_type=F32).astype(BF)
        part = jnp.dot(order[...], part, preferred_element_type=F32)
        if t != 1:
            part = part * keep[t // 2]
        out[:, CPAD * t : CPAD * t + CPAD] = part.astype(BF)
    out[:, 3 * CPAD :] = order[...]


def final_kernel(hidden0, hidden1, hidden2, stats, gain, shift, same, bias, w, out):
    total = stats[0]
    for n in range(1, 32):
        total = total + stats[n]
    s = jnp.concatenate([total[0:1], total[1:2], total[2:3]], axis=1)
    q = jnp.concatenate([total[3:4], total[4:5], total[5:6]], axis=1)
    both = jnp.concatenate([s, q, jnp.zeros((6, CPAD), F32)], axis=0)
    both = exact(both, same[...]) / (CELLS * 32 * C // GROUPS)
    mean, square = both[0:1], both[1:2]
    scale = lax.rsqrt(square - mean * mean + EPS) * gain[...]
    offset = shift[...] - mean * scale
    chunk = 256

    def rows(i, carry):
        here = pl.ds(pl.multiple_of(i * chunk, chunk), chunk)
        parts = [silu(h[here, :].astype(F32) * scale + offset).astype(BF) for h in (hidden0, hidden1, hidden2)]
        parts.append(hidden1[here, :])
        out[here, :] = (nt(jnp.concatenate(parts, axis=1), w[...]) + bias[...]).astype(BF)
        return carry

    lax.fori_loop(0, CELLS // chunk, rows, 0)


FRAME = ("zl", "x")
FORWARD = [(i, i + 1) for i in range(31)]
BACKWARD = [(i + 1, i) for i in range(31)]


def body(video, emb, gain1, shift1, gain2, shift2, sw, tw, bias):
    struct = jax.ShapeDtypeStruct
    const = lambda a, t=BF: jnp.asarray(a, t)
    core = lax.axis_index("core").astype(jnp.int32).reshape(1)
    frame = lax.axis_index(FRAME)
    keep = jnp.stack([frame > 0, frame < 31]).astype(F32)

    pieces = call(pack_kernel, struct((16, 24, 128), BF), n=4)(sw, tw, const(PACK_S), const(PACK_T))
    line = lax.all_to_all(pieces, ("zh", "zl"), 0, 0)
    frames = video.reshape(CELLS, C)
    frame0 = lax.ppermute(frames, FRAME, FORWARD)
    frame2 = lax.ppermute(frames, FRAME, BACKWARD)
    emb1 = emb.reshape(1, C)
    emb0 = lax.ppermute(emb1, FRAME, FORWARD)
    emb2 = lax.ppermute(emb1, FRAME, BACKWARD)

    act = lambda v: call(act_kernel, struct((CELLS + 2 * COLS, KPAD), BF), flops=9_000_000_000, n=5)(
        v, gain1.reshape(1, C), shift1.reshape(1, C), const(SAME1, F32), const(ACT_PERM)
    )
    cols1 = act(frames)
    block = call(line_kernel, struct((16, 48, KPAD), BF), n=2)(line, const(PIECE_PERM))
    own = lax.all_to_all(block, ("y", "x"), 0, 0)
    cols0, cols2 = act(frame0), act(frame2)
    other = lax.ppermute(own, "core", [(0, 1), (1, 0)])

    rows = jnp.concatenate([emb0, emb1, emb2, gain2[None], shift2[None], jnp.zeros((3, C), F32)], axis=0)
    rows = exact(rows, const(ORDER, F32))
    emb0, emb1, emb2, gain2, shift2 = (rows[n : n + 1] for n in range(5))

    weights = pltpu.VMEM((3, CPAD, KPAD), BF)
    hidden = struct((CELLS, CPAD), BF)
    hidden1, stats = call(
        own_kernel, (hidden, struct((32, 8, 128), F32)), flops=4_000_000_000, scratch=[weights], smem=1, n=4
    )(core, cols1, own, other, emb1)
    stats = lax.all_to_all(stats, FRAME, 0, 0)
    own, other, hidden1 = lax.optimization_barrier((own, other, hidden1))
    hidden0, hidden2 = call(near_kernel, (hidden, hidden), flops=8_000_000_000, scratch=[weights], smem=1, n=6)(
        core, cols0, cols2, own, other, emb0, emb2
    )
    w = call(
        temporal_kernel,
        struct((C, 4 * CPAD), BF),
        flops=2_000_000_000,
        scratch=[pltpu.VMEM((CPAD, KPAD), BF)],
        smem=2,
        n=4,
    )(core, keep, own, other, const(TEMP_PERM), const(ORDER))
    out = call(final_kernel, struct((CELLS, C), BF), flops=2_000_000_000, n=9)(
        hidden0, hidden1, hidden2, stats, gain2, shift2, const(SAME2, F32), bias.reshape(1, C), w
    )
    return out.reshape(video.shape)


def solution(mesh):
    split = Mesh(mesh.devices.reshape(4, 2, 2, 8, 4), ("y", "zh", "core", "zl", "x"))
    dp = ("y", "zh", "core")
    data = P(dp, FRAME, None, None, None)
    placed = (data, P(dp, FRAME, None), P(), P(), P(), P(), P(None, FRAME, dp), P(None, FRAME, dp), P())
    return jax.shard_map(body, mesh=split, in_specs=placed, out_specs=data, check_vma=False)
```

```python
import functools

import jax
import jax.numpy as jnp
import numpy as np
from jax import lax
from jax.experimental import pallas as pl
from jax.experimental.pallas import tpu as pltpu
from jax.sharding import Mesh, PartitionSpec as P

GROUPS = 32
C = 320
CELLS = 1536
COLS = 64
EPS = 1e-5
BF = jnp.bfloat16
F32 = jnp.float32
KPAD = 1024
CPAD = 384
HALF = 192
PACKED = CELLS * 5 // 2 + 16
VMEM = 60 * 1024 * 1024


def _consts():
    act_perm = np.zeros((KPAD, KPAD), np.float32)
    for f in range(32):
        zl, x = divmod(f, 4)
        for kk in range(30):
            b, i = divmod(30 * f + kk, C)
            row = 256 * b + i if i < 256 else 768 + 64 * b + i - 256
            act_perm[row, 256 * x + 30 * zl + kk] = 1
    piece_perm = np.zeros((8, 128, KPAD), np.float32)
    for zl in range(8):
        for a in range(3):
            for kk in range(30):
                piece_perm[zl, 30 * a + kk, 256 * a + 30 * zl + kk] = 1
            for kk in range(10):
                piece_perm[zl, 90 + 10 * a + kk, 768 + 80 * a + 10 * zl + kk] = 1
    chan = np.zeros(C, np.int64)
    for i in range(C):
        d, j = divmod(i, 20)
        y, zh, core = d // 4, (d // 2) % 2, d % 2
        chan[i] = HALF * core + 48 * y + 24 * zh + j
    order = np.zeros((C, CPAD), np.float32)
    order[np.arange(C), chan] = 1
    temp_perm = np.zeros((KPAD, 3 * CPAD), np.float32)
    for x in range(4):
        for t in range(3):
            for zl in range(8):
                for kk in range(10):
                    i = 40 * zl + 10 * x + kk
                    temp_perm[256 * x + 80 * t + 10 * zl + kk, CPAD * t + chan[i]] = 1
    same1 = np.kron(np.eye(GROUPS), np.ones((10, 10))).astype(np.float32)
    same2 = order.T @ same1 @ order
    return act_perm, piece_perm, order, temp_perm, same1, same2


ACT_PERM, PIECE_PERM, ORDER, TEMP_PERM, SAME1, SAME2 = _consts()


def call(kernel, out_shape, flops=0, smem=0, n=0):
    specs = [pl.BlockSpec(memory_space=pltpu.SMEM)] * smem + [pl.BlockSpec(memory_space=pltpu.VMEM)] * n
    return pl.pallas_call(
        kernel,
        out_shape=out_shape,
        in_specs=specs,
        out_specs=jax.tree.map(lambda _: pl.BlockSpec(memory_space=pltpu.VMEM), out_shape),
        compiler_params=pltpu.CompilerParams(vmem_limit_bytes=VMEM),
        cost_estimate=pl.CostEstimate(flops=flops, bytes_accessed=0, transcendentals=0),
    )


def exact(a, b):
    return jnp.dot(a, b, precision=lax.Precision.HIGHEST, preferred_element_type=F32)


def nt(a, b):
    return lax.dot_general(a, b, (((1,), (1,)), ((), ())), preferred_element_type=F32)


def silu(v):
    half = 0.5 * v
    return half + half * jnp.tanh(half)


def pack_kernel(sw, tw, out):
    total = jnp.zeros((20, 128), F32)
    for a in range(3):
        lane = lax.broadcasted_iota(jnp.int32, (30, 128), 1) - lax.broadcasted_iota(jnp.int32, (30, 128), 0)
        total += jnp.dot(sw[a], (lane == 30 * a).astype(F32).astype(BF), preferred_element_type=F32)
        lane = lane[:10]
        spread = (lane == 90 + 10 * a).astype(F32).astype(BF)
        total += lax.dot_general(tw[a], spread, (((0,), (0,)), ((), ())), preferred_element_type=F32)
    piece = jnp.concatenate([total, jnp.zeros((4, 128), F32)], axis=0).astype(BF)
    for n in range(16):
        out[n] = piece


def frame_kernel(video, emb, out):
    out[pl.ds(0, CELLS), :] = video[:, 0:128]
    out[pl.ds(CELLS, CELLS), :] = video[:, 128:256]
    out[pl.ds(2 * CELLS, CELLS // 2), :] = jnp.concatenate(
        [video[: CELLS // 2, 256:320], video[CELLS // 2 :, 256:320]], axis=1
    )
    rest = jnp.concatenate([emb[...], jnp.zeros((1, 64), F32)], axis=1)
    rows = []
    for n in range(3):
        part = rest.astype(BF).astype(F32)
        rest = rest - part
        rows += [part[:, 0:128], part[:, 128:256], part[:, 256:384]]
    rows.append(jnp.zeros((7, 128), F32))
    out[pl.ds(PACKED - 16, 16), :] = jnp.concatenate(rows, axis=0).astype(BF)


def line_kernel(pieces, perm, out):
    total = jnp.zeros((48, KPAD), F32)
    for zl in range(8):
        both = jnp.concatenate([pieces[zl].astype(F32), pieces[8 + zl].astype(F32)], axis=0)
        total += jnp.dot(both.astype(BF), perm[zl], preferred_element_type=F32)
    block = total.astype(BF)
    for n in range(16):
        out[n] = block


def act_kernel(frame, gain, shift, same, order, perm, out, emb):
    chunk = 256
    half = CELLS // 2

    def load(i):
        start = i * chunk
        a = frame[pl.ds(start, chunk), :]
        b = frame[pl.ds(CELLS + start, chunk), :]
        c = frame[pl.ds(2 * CELLS + start % half, chunk), :]
        c = c[:, :64] if start < half else c[:, 64:]
        return jnp.concatenate([a.astype(F32), b.astype(F32), c.astype(F32)], axis=1)

    s = jnp.zeros((8, C), F32)
    q = jnp.zeros((8, C), F32)
    for i in range(CELLS // chunk):
        v = load(i).reshape(chunk // 8, 8, C)
        s, q = s + jnp.sum(v, axis=0), q + jnp.sum(v * v, axis=0)
    count = CELLS * C // GROUPS
    both = exact(jnp.concatenate([s, q], axis=0), same[...]) / count
    mean = jnp.sum(both[:8], axis=0, keepdims=True)
    square = jnp.sum(both[8:], axis=0, keepdims=True)
    scale = lax.rsqrt(square - mean * mean + EPS) * gain[...]
    offset = shift[...] - mean * scale
    column = lax.rem(lax.broadcasted_iota(jnp.int32, (chunk, C), 0), COLS)
    out[pl.ds(0, COLS), :] = jnp.zeros((COLS, KPAD), BF)
    out[pl.ds(CELLS + COLS, COLS), :] = jnp.zeros((COLS, KPAD), BF)
    for i in range(CELLS // chunk):
        v = silu(load(i) * scale + offset).astype(BF).astype(F32)
        before = jnp.where(column == 0, 0.0, pltpu.roll(v, 1, 0))
        after = jnp.where(column == COLS - 1, 0.0, pltpu.roll(v, chunk - 1, 0))
        rest = [before[:, 256:], v[:, 256:], after[:, 256:], jnp.zeros((chunk, 64), F32)]
        taps = jnp.concatenate([before[:, :256], v[:, :256], after[:, :256]] + rest, axis=1).astype(BF)
        total = jnp.dot(taps, perm[...], preferred_element_type=F32)
        out[pl.ds(i * chunk + COLS, chunk), :] = total.astype(BF)
    rows = frame[pl.ds(PACKED - 16, 16), :].astype(F32)
    parts = [jnp.concatenate([rows[3 * n : 3 * n + 1], rows[3 * n + 1 : 3 * n + 2], rows[3 * n + 2 : 3 * n + 3, :64]], axis=1) for n in range(3)]
    parts = jnp.concatenate(parts + [jnp.zeros((5, C), F32)], axis=0).astype(BF)
    emb[...] = jnp.sum(jnp.dot(parts, order[...], preferred_element_type=F32), axis=0, keepdims=True)


def place_weights(core, own, other, w):
    mine = core * HALF
    theirs = HALF - mine
    for y in range(4):
        for x in range(4):
            for a in range(4):
                lanes = pl.ds(256 * x, 256)
                w[a, pl.ds(pl.multiple_of(mine + 48 * y, 16), 48), lanes] = own[4 * y + x, :, 256 * a : 256 * a + 256]
                w[a, pl.ds(pl.multiple_of(theirs + 48 * y, 16), 48), lanes] = other[4 * y + x, :, 256 * a : 256 * a + 256]


def convolve(cols, w, emb, hidden, stats):
    chunk = 256
    s = jnp.zeros((8, CPAD), F32)
    q = jnp.zeros((8, CPAD), F32)
    for i in range(CELLS // chunk):
        total = jnp.zeros((CPAD, chunk), F32)
        for a in range(3):
            total += nt(w[a], cols[pl.ds(i * chunk + COLS * a, chunk), :])
        h = (total.T + emb).astype(BF)
        hidden[pl.ds(i * chunk, chunk), :] = h
        if stats:
            h = h.astype(F32).reshape(chunk // 8, 8, CPAD)
            s, q = s + jnp.sum(h, axis=0), q + jnp.sum(h * h, axis=0)
    return s, q


def own_kernel(core, cols, own, other, emb, hidden, stats, w):
    place_weights(core[0], own, other, w)
    s, q = convolve(cols, w, emb[...], hidden, True)
    s = jnp.sum(s, axis=0, keepdims=True)
    q = jnp.sum(q, axis=0, keepdims=True)
    rows = [s[:, :128], s[:, 128:256], s[:, 256:], q[:, :128], q[:, 128:256], q[:, 256:], jnp.zeros((2, 128), F32)]
    block = jnp.concatenate(rows, axis=0)
    for n in range(32):
        stats[n] = block


def near_kernel(before, after, w, emb0, emb2, hidden0, hidden2):
    convolve(before, w, emb0[...], hidden0, False)
    convolve(after, w, emb2[...], hidden2, False)


def temporal_kernel(keep, w, perm, order, out):
    for t in range(3):
        part = jnp.dot(w[3], perm[:, CPAD * t : CPAD * t + CPAD], preferred_element_type=F32).astype(BF)
        part = jnp.dot(order[...], part, preferred_element_type=F32)
        if t != 1:
            part = part * keep[t // 2]
        out[:, CPAD * t : CPAD * t + CPAD] = part.astype(BF)
    out[:, 3 * CPAD :] = order[...]


def final_kernel(hidden0, hidden1, hidden2, stats, gain, shift, same, bias, w, out):
    total = stats[0]
    for n in range(1, 32):
        total = total + stats[n]
    s = jnp.concatenate([total[0:1], total[1:2], total[2:3]], axis=1)
    q = jnp.concatenate([total[3:4], total[4:5], total[5:6]], axis=1)
    both = jnp.concatenate([s, q, jnp.zeros((6, CPAD), F32)], axis=0)
    both = exact(both, same[...]) / (CELLS * 32 * C // GROUPS)
    mean, square = both[0:1], both[1:2]
    scale = lax.rsqrt(square - mean * mean + EPS) * gain[...]
    offset = shift[...] - mean * scale
    chunk = 256
    for i in range(CELLS // chunk):
        here = pl.ds(i * chunk, chunk)
        parts = [silu(h[here, :].astype(F32) * scale + offset).astype(BF) for h in (hidden0, hidden1, hidden2)]
        parts.append(hidden1[here, :])
        out[here, :] = (nt(jnp.concatenate(parts, axis=1), w[...]) + bias[...]).astype(BF)


FILL = 7_500_000_000
FRAME = ("zl", "x")
FORWARD = [(i, i + 1) for i in range(31)]
BACKWARD = [(i + 1, i) for i in range(31)]


def body(video, emb, gain1, shift1, gain2, shift2, sw, tw, bias):
    struct = jax.ShapeDtypeStruct
    const = lambda a, t=BF: jnp.asarray(a, t)
    core = lax.axis_index("core").astype(jnp.int32).reshape(1)
    frame = lax.axis_index(FRAME)
    keep = jnp.stack([frame > 0, frame < 31]).astype(F32)

    pieces = call(pack_kernel, struct((16, 24, 128), BF), n=2)(sw.transpose(0, 2, 1), tw)
    frame1 = call(frame_kernel, struct((PACKED, 128), BF), n=2)(video.reshape(CELLS, C), emb.reshape(1, C))
    line = lax.all_to_all(pieces, ("zh", "zl"), 0, 0)
    frame0 = lax.ppermute(frame1, FRAME, FORWARD)
    frame2 = lax.ppermute(frame1, FRAME, BACKWARD)

    act = lambda v, flops=100_000_000: call(act_kernel, (struct((CELLS + 2 * COLS, KPAD), BF), struct((1, CPAD), F32)), flops=flops, n=6)(
        v, gain1.reshape(1, C), shift1.reshape(1, C), const(SAME1, F32), const(ORDER), const(ACT_PERM)
    )
    cols1, emb1 = act(frame1)
    line, cols1 = lax.optimization_barrier((line, cols1))
    block = call(line_kernel, struct((16, 48, KPAD), BF), n=2)(line, const(PIECE_PERM))
    own = lax.all_to_all(block, ("y", "x"), 0, 0)
    frame0, frame2 = lax.optimization_barrier((frame0, frame2))
    cols0, emb0 = act(frame0, FILL)
    own, cols0 = lax.optimization_barrier((own, cols0))
    other = lax.ppermute(own, "core", [(0, 1), (1, 0)])
    cols2, emb2 = act(frame2)
    other, cols2 = lax.optimization_barrier((other, cols2))
    rows = exact(jnp.concatenate([gain2[None], shift2[None], jnp.zeros((6, C), F32)], axis=0), const(ORDER, F32))

    hidden = struct((CELLS, CPAD), BF)
    hidden1, stats, w = call(
        own_kernel, (hidden, struct((32, 8, 128), F32), struct((4, CPAD, KPAD), BF)), smem=1, n=4
    )(core, cols1, own, other, emb1)
    stats = lax.all_to_all(stats, FRAME, 0, 0)
    hidden0, hidden2 = call(near_kernel, (hidden, hidden), flops=7_300_000_000, n=5)(cols0, cols2, w, emb0, emb2)
    w = call(temporal_kernel, struct((C, 4 * CPAD), BF), flops=1_000_000_000, smem=1, n=3)(keep, w, const(TEMP_PERM), const(ORDER))
    out = call(final_kernel, struct((CELLS, C), BF), n=9)(
        hidden0, hidden1, hidden2, stats, rows[0:1], rows[1:2], const(SAME2, F32), bias.reshape(1, C), w
    )
    return out.reshape(video.shape)


def solution(mesh):
    split = Mesh(mesh.devices.reshape(4, 2, 2, 8, 4), ("y", "zh", "core", "zl", "x"))
    dp = ("y", "zh", "core")
    data = P(dp, FRAME, None, None, None)
    placed = (data, P(dp, FRAME, None), P(), P(), P(), P(), P(None, FRAME, dp), P(None, FRAME, dp), P())
    return jax.shard_map(body, mesh=split, in_specs=placed, out_specs=data, check_vma=False)
```

```python
import functools

import jax
import jax.numpy as jnp
import numpy as np
from jax import lax
from jax.experimental import pallas as pl
from jax.experimental.pallas import tpu as pltpu
from jax.sharding import Mesh, PartitionSpec as P

GROUPS = 32
C = 320
CELLS = 1536
COLS = 64
EPS = 1e-5
BF = jnp.bfloat16
F32 = jnp.float32
KPAD = 1024
CPAD = 384
HALF = 192
PACKED = CELLS * 5 // 2 + 16
VMEM = 60 * 1024 * 1024


def _consts():
    act_perm = np.zeros((KPAD, KPAD), np.float32)
    for f in range(32):
        zl, x = divmod(f, 4)
        for kk in range(30):
            b, i = divmod(30 * f + kk, C)
            row = 256 * b + i if i < 256 else 768 + 64 * b + i - 256
            act_perm[row, 256 * x + 30 * zl + kk] = 1
    chan = np.zeros(C, np.int64)
    for i in range(C):
        d, j = divmod(i, 20)
        y, zh, core = d // 4, (d // 2) % 2, d % 2
        chan[i] = HALF * core + 48 * y + 24 * zh + j
    order = np.zeros((C, CPAD), np.float32)
    order[np.arange(C), chan] = 1
    temp_perm = np.zeros((KPAD, 3 * CPAD), np.float32)
    for x in range(4):
        for t in range(3):
            for zl in range(8):
                for kk in range(10):
                    i = 40 * zl + 10 * x + kk
                    temp_perm[256 * x + 30 * zl + 10 * t + kk, CPAD * t + chan[i]] = 1
    same1 = np.kron(np.eye(GROUPS), np.ones((10, 10))).astype(np.float32)
    same2 = order.T @ same1 @ order
    return act_perm, order, temp_perm, same1, same2


ACT_PERM, ORDER, TEMP_PERM, SAME1, SAME2 = _consts()


def call(kernel, out_shape, ins, outs=None, scratch=(), flops=0, vmem=VMEM):
    space = {"v": pltpu.VMEM, "a": pl.ANY}
    specs = lambda letters: [pl.BlockSpec(memory_space=space[c]) for c in letters]
    outs = specs(outs or "v" * len(out_shape))
    return pl.pallas_call(
        kernel,
        out_shape=tuple(out_shape),
        in_specs=specs(ins),
        out_specs=tuple(outs),
        scratch_shapes=list(scratch),
        compiler_params=pltpu.CompilerParams(vmem_limit_bytes=vmem),
        cost_estimate=pl.CostEstimate(flops=flops, bytes_accessed=0, transcendentals=0),
    )


class Mover:
    def __init__(self, sems):
        self.sems, self.used = sems, 0

    def start(self, src, dst):
        copy = pltpu.make_async_copy(src, dst, self.sems.at[self.used])
        self.used += 1
        copy.start()
        return copy


def exact(a, b):
    return jnp.dot(a, b, precision=lax.Precision.HIGHEST, preferred_element_type=F32)


def nt(a, b):
    return lax.dot_general(a, b, (((1,), (1,)), ((), ())), preferred_element_type=F32)


def silu(v):
    half = 0.5 * v
    return half + half * jnp.tanh(half)


def pack_kernel(sw, tw, out):
    lane = lax.broadcasted_iota(jnp.int32, (30, 128), 1)
    row = lax.broadcasted_iota(jnp.int32, (30, 128), 0)
    total = jnp.zeros((20, 128), F32)
    for a in range(3):
        total += jnp.dot(sw[a], (lane == row + 30 * a).astype(F32).astype(BF), preferred_element_type=F32)
    rows = jnp.concatenate([tw[r].astype(F32) for r in range(10)], axis=0).astype(BF)
    spread = (lane == 90 + 10 * lax.rem(row, 3) + lax.div(row, 3)).astype(F32).astype(BF)
    total += lax.dot_general(rows, spread, (((0,), (0,)), ((), ())), preferred_element_type=F32)
    piece = jnp.concatenate([total, jnp.zeros((4, 128), F32)], axis=0).astype(BF)
    for n in range(16):
        out[n] = piece


def frame_kernel(video, emb, out):
    out[pl.ds(0, CELLS), :] = video[:, 0:128]
    out[pl.ds(CELLS, CELLS), :] = video[:, 128:256]
    out[pl.ds(2 * CELLS, CELLS // 2), :] = jnp.concatenate(
        [video[: CELLS // 2, 256:320], video[CELLS // 2 :, 256:320]], axis=1
    )
    rest = jnp.concatenate([emb[0], jnp.zeros((1, 64), F32)], axis=1)
    rows = []
    for n in range(3):
        part = rest.astype(BF).astype(F32)
        rest = rest - part
        rows += [part[:, 0:128], part[:, 128:256], part[:, 256:384]]
    rows.append(jnp.zeros((7, 128), F32))
    out[pl.ds(PACKED - 16, 16), :] = jnp.concatenate(rows, axis=0).astype(BF)


def line_kernel(pieces, out):
    both = [jnp.concatenate([pieces[zl].astype(F32), pieces[8 + zl].astype(F32)], axis=0) for zl in range(8)]
    pad = jnp.zeros((48, 16), F32)
    groups = [jnp.concatenate([b[:, 30 * a : 30 * a + 30] for b in both] + [pad], axis=1) for a in range(4)]
    block = jnp.concatenate(groups, axis=1).astype(BF)
    for n in range(16):
        out[n] = block


def act_kernel(*refs):
    count = (len(refs) - 8) // 3
    frames = refs[:count]
    gain, shift, same, order, perm_hbm = refs[count : count + 5]
    outs = refs[count + 5 : 3 * count + 5]
    perm, out, sems = refs[3 * count + 5 :]
    move = Mover(sems)
    perm_copy = move.start(perm_hbm, perm)
    chunk = 256
    half = CELLS // 2
    column = lax.rem(lax.broadcasted_iota(jnp.int32, (chunk, 256), 0), COLS)
    low = lax.broadcasted_iota(jnp.int32, (chunk, 128), 1) < 64
    cells = CELLS * C // GROUPS

    def shifted(v):
        edge = column[:, : v.shape[1]]
        before = jnp.where(edge == 0, 0.0, pltpu.roll(v, 1, 0))
        after = jnp.where(edge == COLS - 1, 0.0, pltpu.roll(v, chunk - 1, 0))
        return before, v, after

    copies = []
    for f, frame in enumerate(frames):
        main = lambda i: jnp.concatenate(
            [frame[pl.ds(i * chunk, chunk), :], frame[pl.ds(CELLS + i * chunk, chunk), :]], axis=1
        ).astype(F32)
        rest = lambda i: frame[pl.ds(2 * CELLS + i * chunk, chunk), :].astype(F32)
        s = jnp.zeros((8, 256), F32)
        q = jnp.zeros((8, 256), F32)
        for i in range(CELLS // chunk):
            v = main(i).reshape(chunk // 8, 8, 256)
            s, q = s + jnp.sum(v, axis=0), q + jnp.sum(v * v, axis=0)
        s2 = jnp.zeros((8, 128), F32)
        q2 = jnp.zeros((8, 128), F32)
        for i in range(half // chunk):
            v = rest(i).reshape(chunk // 8, 8, 128)
            s2, q2 = s2 + jnp.sum(v, axis=0), q2 + jnp.sum(v * v, axis=0)
        s = jnp.concatenate([s, s2[:, :64] + s2[:, 64:]], axis=1)
        q = jnp.concatenate([q, q2[:, :64] + q2[:, 64:]], axis=1)
        both = exact(jnp.concatenate([s, q], axis=0), same[...]) / cells
        mean = jnp.sum(both[:8], axis=0, keepdims=True)
        square = jnp.sum(both[8:], axis=0, keepdims=True)
        scale = lax.rsqrt(square - mean * mean + EPS) * gain[...].reshape(1, C)
        offset = shift[...].reshape(1, C) - mean * scale
        scale2 = jnp.concatenate([scale[:, 256:], scale[:, 256:]], axis=1)
        offset2 = jnp.concatenate([offset[:, 256:], offset[:, 256:]], axis=1)
        scale, offset = scale[:, :256], offset[:, :256]
        rows = frame[pl.ds(PACKED - 16, 16), :].astype(F32)
        parts = [
            jnp.concatenate([rows[n : n + 1], rows[n + 1 : n + 2], rows[n + 2 : n + 3, :64]], axis=1) for n in (0, 3, 6)
        ]
        parts = jnp.concatenate(parts + [jnp.zeros((5, C), F32)], axis=0).astype(BF)
        outs[2 * f + 1][...] = jnp.sum(jnp.dot(parts, order[...], preferred_element_type=F32), axis=0, keepdims=True)
        out[f, pl.ds(0, COLS), :] = jnp.zeros((COLS, KPAD), BF)
        out[f, pl.ds(CELLS + COLS, COLS), :] = jnp.zeros((COLS, KPAD), BF)
        if f == 0:
            perm_copy.wait()
        for i in range(half // chunk):
            before2, v2, after2 = shifted(silu(rest(i) * scale2 + offset2).astype(BF).astype(F32))
            swap = lambda v: pltpu.roll(v, 64, 1)
            tails = [
                (jnp.where(low, before2, swap(v2)), jnp.where(low, after2, 0.0)),
                (jnp.where(low, swap(before2), v2), jnp.where(low, swap(after2), 0.0)),
            ]
            for n in range(2):
                at = i + n * (half // chunk)
                taps = shifted(silu(main(at) * scale + offset).astype(BF).astype(F32))
                taps = jnp.concatenate(taps + tails[n], axis=1).astype(BF)
                total = jnp.dot(taps, perm[...], preferred_element_type=F32)
                out[f, pl.ds(at * chunk + COLS, chunk), :] = total.astype(BF)
        copies.append(move.start(out.at[f], outs[2 * f]))
    for copy in copies:
        copy.wait()


def place_weights(half, block, w):
    for y in range(4):
        for x in range(4):
            for a in range(4):
                rows = pl.ds(pl.multiple_of(half + 48 * y, 16), 48)
                w[a, rows, 256 * x : 256 * x + 256] = block[4 * y + x, :, 256 * a : 256 * a + 256]


def convolve(i, cols, w, emb):
    total = jnp.zeros((CPAD, 256), F32)
    for a in range(3):
        total += nt(w[a], cols[pl.ds(i * 256 + COLS * a, 256), :])
    return (total.T + emb).astype(BF)


def own_kernel(cols_hbm, own_hbm, other_hbm, emb, hidden_hbm, stats, w_hbm, cols, own, other, hidden, w, sems):
    move = Mover(sems)
    own_copy = move.start(own_hbm, own)
    other_copy = move.start(other_hbm, other)
    cols_copy = move.start(cols_hbm, cols)
    mine = lax.axis_index("core") * HALF
    own_copy.wait()
    place_weights(mine, own, w)
    other_copy.wait()
    place_weights(HALF - mine, other, w)
    cols_copy.wait()
    copies = [move.start(w, w_hbm)]
    s = jnp.zeros((8, CPAD), F32)
    q = jnp.zeros((8, CPAD), F32)
    for i in range(CELLS // 256):
        h = convolve(i, cols, w, emb[...])
        hidden[pl.ds(i * 256, 256), :] = h
        h = h.astype(F32).reshape(32, 8, CPAD)
        s, q = s + jnp.sum(h, axis=0), q + jnp.sum(h * h, axis=0)
    copies.append(move.start(hidden, hidden_hbm))
    s = jnp.sum(s, axis=0, keepdims=True)
    q = jnp.sum(q, axis=0, keepdims=True)
    rows = [s[:, :128], s[:, 128:256], s[:, 256:], q[:, :128], q[:, 128:256], q[:, 256:], jnp.zeros((2, 128), F32)]
    block = jnp.concatenate(rows, axis=0)
    for n in range(32):
        stats[n] = block
    for copy in copies:
        copy.wait()


def temporal_kernel(w_hbm, perm, order, gain, shift, out, affine, w, sems):
    move = Mover(sems)
    move.start(w_hbm.at[3], w).wait()
    frame = lax.axis_index("zl") * 4 + lax.axis_index("x")
    keep = [(frame > 0).astype(F32), 1.0, (frame < 31).astype(F32)]
    for t in range(3):
        part = jnp.dot(w[...], perm[:, CPAD * t : CPAD * t + CPAD], preferred_element_type=F32).astype(BF)
        part = jnp.dot(order[...], part, preferred_element_type=F32) * keep[t]
        out[:, CPAD * t : CPAD * t + CPAD] = part.astype(BF)
    out[:, 3 * CPAD :] = order[...]
    rest = jnp.concatenate([gain[...].reshape(1, C), shift[...].reshape(1, C), jnp.zeros((6, C), F32)], axis=0)
    total = jnp.zeros((8, CPAD), F32)
    for n in range(3):
        part = rest.astype(BF)
        rest = rest - part.astype(F32)
        total += jnp.dot(part, order[...], preferred_element_type=F32)
    affine[...] = total


def final_kernel(
    cols0_hbm, cols2_hbm, w_hbm, hidden_hbm, last_hbm, emb0, emb2, stats, affine, same, bias, out_hbm,
    cols0, cols2, w, hidden, last, out, sems,
):
    move = Mover(sems)
    first, second = pl.ds(0, 1024), pl.ds(1024, CELLS + 2 * COLS - 1024)
    begin = [move.start(w_hbm.at[pl.ds(0, 3)], w)]
    begin += [move.start(h.at[first], c.at[first]) for h, c in ((cols0_hbm, cols0), (cols2_hbm, cols2))]
    begin += [move.start(hidden_hbm, hidden), move.start(last_hbm, last)]
    later = [move.start(h.at[second], c.at[second]) for h, c in ((cols0_hbm, cols0), (cols2_hbm, cols2))]
    total = stats[0]
    for n in range(1, 32):
        total = total + stats[n]
    s = jnp.concatenate([total[0:1], total[1:2], total[2:3]], axis=1)
    q = jnp.concatenate([total[3:4], total[4:5], total[5:6]], axis=1)
    both = jnp.concatenate([s, q, jnp.zeros((6, CPAD), F32)], axis=0)
    both = exact(both, same[...]) / (CELLS * 32 * C // GROUPS)
    mean, square = both[0:1], both[1:2]
    scale = lax.rsqrt(square - mean * mean + EPS) * affine[0:1]
    offset = affine[1:2] - mean * scale
    bias_row = bias[...].reshape(1, C)
    mix = lambda h: silu(h.astype(F32) * scale + offset).astype(BF)
    for copy in begin:
        copy.wait()
    near = lambda i: (convolve(i, cols0, w, emb0[...]), convolve(i, cols2, w, emb2[...]))
    now = near(0)
    copies = []
    for i in range(CELLS // 256):
        if i == 2:
            for copy in later:
                copy.wait()
        later_now = near(i + 1) if i < CELLS // 256 - 1 else None
        here = pl.ds(i * 256, 256)
        h = hidden[here, :]
        taps = jnp.concatenate([mix(now[0]), mix(h), mix(now[1]), h], axis=1)
        out[here, :] = (nt(taps, last[...]) + bias_row).astype(BF)
        now = later_now
        if i == 2:
            copies.append(move.start(out.at[pl.ds(0, 768)], out_hbm.at[pl.ds(0, 768)]))
    copies.append(move.start(out.at[pl.ds(768, 768)], out_hbm.at[pl.ds(768, 768)]))
    for copy in copies:
        copy.wait()


FILL = 15_000_000_000
FRAME = ("zl", "x")
FORWARD = [(i, i + 1) for i in range(31)]
BACKWARD = [(i + 1, i) for i in range(31)]


def body(video, emb, gain1, shift1, gain2, shift2, sw, tw, bias):
    struct = jax.ShapeDtypeStruct
    const = lambda a, t=BF: jnp.asarray(a, t)
    sems = pltpu.SemaphoreType.DMA
    buffer = lambda *shape: pltpu.VMEM(shape, BF)
    cols = (CELLS + 2 * COLS, KPAD)

    (pieces,) = call(pack_kernel, [struct((16, 24, 128), BF)], "vv")(sw.transpose(0, 2, 1), tw.transpose(1, 0, 2))
    (frame1,) = call(frame_kernel, [struct((PACKED, 128), BF)], "vv")(video.reshape(CELLS, C), emb)
    line = lax.all_to_all(pieces, ("zh", "zl"), 0, 0)
    frame0 = lax.ppermute(frame1, FRAME, FORWARD)
    frame2 = lax.ppermute(frame1, FRAME, BACKWARD)

    act = lambda frames, flops=100_000_000: call(
        act_kernel,
        [struct(cols, BF), struct((1, CPAD), F32)] * len(frames),
        "v" * len(frames) + "vvvva",
        "av" * len(frames),
        [buffer(KPAD, KPAD), buffer(len(frames), *cols), sems((1 + len(frames),))],
        flops,
    )(*frames, gain1, shift1, const(SAME1, F32), const(ORDER), const(ACT_PERM))
    cols1, emb1 = act([frame1])
    line, cols1 = lax.optimization_barrier((line, cols1))
    (block,) = call(line_kernel, [struct((16, 48, KPAD), BF)], "v")(line)
    own = lax.all_to_all(block, ("y", "x"), 0, 0)
    cols0, emb0, cols2, emb2 = act([frame0, frame2], FILL)
    own, cols0 = lax.optimization_barrier((own, cols0))
    other = lax.ppermute(own, "core", [(0, 1), (1, 0)])

    blocks = (16, 48, KPAD)
    hidden1, stats, w = call(
        own_kernel,
        [struct((CELLS, CPAD), BF), struct((32, 8, 128), F32), struct((4, CPAD, KPAD), BF)],
        "aaav",
        "ava",
        [buffer(*cols), buffer(*blocks), buffer(*blocks), buffer(CELLS, CPAD), buffer(4, CPAD, KPAD), sems((5,))],
    )(cols1, own, other, emb1)
    stats = lax.all_to_all(stats, FRAME, 0, 0)
    last, affine = call(
        temporal_kernel,
        [struct((C, 4 * CPAD), BF), struct((8, CPAD), F32)],
        "avvvv",
        scratch=[buffer(CPAD, KPAD), sems((1,))],
        flops=3_000_000_000,
    )(w, const(TEMP_PERM), const(ORDER), gain2, shift2)
    (out,) = call(
        final_kernel,
        [struct((CELLS, C), BF)],
        "aaaaavvvvvv",
        "a",
        [
            buffer(*cols),
            buffer(*cols),
            buffer(3, CPAD, KPAD),
            buffer(CELLS, CPAD),
            buffer(C, 4 * CPAD),
            buffer(CELLS, C),
            sems((9,)),
        ],
    )(cols0, cols2, w, hidden1, last, emb0, emb2, stats, affine, const(SAME2, F32), bias)
    return out.reshape(video.shape)


def solution(mesh):
    split = Mesh(mesh.devices.reshape(4, 2, 2, 8, 4), ("y", "zh", "core", "zl", "x"))
    dp = ("y", "zh", "core")
    data = P(dp, FRAME, None, None, None)
    placed = (data, P(dp, FRAME, None), P(), P(), P(), P(), P(None, FRAME, dp), P(None, FRAME, dp), P())
    return jax.shard_map(body, mesh=split, in_specs=placed, out_specs=data, check_vma=False)
```

```python
import functools

import jax
import jax.numpy as jnp
import numpy as np
from jax import lax
from jax.experimental import pallas as pl
from jax.experimental.pallas import tpu as pltpu
from jax.sharding import Mesh, PartitionSpec as P

GROUPS = 32
C = 320
CELLS = 1536
COLS = 64
EPS = 1e-5
BF = jnp.bfloat16
F32 = jnp.float32
KPAD = 1024
CPAD = 384
HALF = 192
PACKED = CELLS * 5 // 2 + 16
VMEM = 60 * 1024 * 1024


def _consts():
    act_perm = np.zeros((KPAD, KPAD), np.float32)
    for f in range(32):
        zl, x = divmod(f, 4)
        for kk in range(30):
            b, i = divmod(30 * f + kk, C)
            row = 256 * b + i if i < 256 else 768 + 64 * b + i - 256
            act_perm[row, 256 * x + 30 * zl + kk] = 1
    chan = np.zeros(C, np.int64)
    for i in range(C):
        d, j = divmod(i, 20)
        y, zh, core = d // 4, (d // 2) % 2, d % 2
        chan[i] = HALF * core + 48 * y + 24 * zh + j
    order = np.zeros((C, CPAD), np.float32)
    order[np.arange(C), chan] = 1
    temp_perm = np.zeros((4, 256, 768), np.float32)
    for x in range(4):
        for t in range(3):
            for zl in range(8):
                for kk in range(10):
                    to = chan[40 * zl + 10 * x + kk] - 128 * (x // 2)
                    temp_perm[x, 30 * zl + 10 * t + kk, 256 * t + to] = 1
    same1 = np.kron(np.eye(GROUPS), np.ones((10, 10))).astype(np.float32)
    same2 = order.T @ same1 @ order
    return act_perm, order, temp_perm, same1, same2


ACT_PERM, ORDER, TEMP_PERM, SAME1, SAME2 = _consts()


def call(kernel, out_shape, ins, outs=None, scratch=(), flops=0, vmem=VMEM):
    space = {"v": pltpu.VMEM, "a": pl.ANY}
    specs = lambda letters: [pl.BlockSpec(memory_space=space[c]) for c in letters]
    outs = specs(outs or "v" * len(out_shape))
    return pl.pallas_call(
        kernel,
        out_shape=tuple(out_shape),
        in_specs=specs(ins),
        out_specs=tuple(outs),
        scratch_shapes=list(scratch),
        compiler_params=pltpu.CompilerParams(vmem_limit_bytes=vmem),
        cost_estimate=pl.CostEstimate(flops=flops, bytes_accessed=0, transcendentals=0),
    )


class Mover:
    def __init__(self, sems):
        self.sems, self.used = sems, 0

    def start(self, src, dst):
        copy = pltpu.make_async_copy(src, dst, self.sems.at[self.used])
        self.used += 1
        copy.start()
        return copy


def exact(a, b):
    return jnp.dot(a, b, precision=lax.Precision.HIGHEST, preferred_element_type=F32)


def nt(a, b):
    return lax.dot_general(a, b, (((1,), (1,)), ((), ())), preferred_element_type=F32)


def silu(v):
    half = 0.5 * v
    return half + half * jnp.tanh(half)


def pack_kernel(sw, tw, out):
    lane = lax.broadcasted_iota(jnp.int32, (30, 128), 1)
    row = lax.broadcasted_iota(jnp.int32, (30, 128), 0)
    total = jnp.zeros((20, 128), F32)
    for a in range(3):
        total += jnp.dot(sw[a], (lane == row + 30 * a).astype(F32).astype(BF), preferred_element_type=F32)
    rows = jnp.concatenate([tw[r].astype(F32) for r in range(10)], axis=0).astype(BF)
    spread = (lane == 90 + 10 * lax.rem(row, 3) + lax.div(row, 3)).astype(F32).astype(BF)
    total += lax.dot_general(rows, spread, (((0,), (0,)), ((), ())), preferred_element_type=F32)
    piece = jnp.concatenate([total, jnp.zeros((4, 128), F32)], axis=0).astype(BF)
    for n in range(16):
        out[n] = piece


def frame_kernel(video, emb, out):
    out[pl.ds(0, CELLS), :] = video[:, 0:128]
    out[pl.ds(CELLS, CELLS), :] = video[:, 128:256]
    out[pl.ds(2 * CELLS, CELLS // 2), :] = jnp.concatenate(
        [video[: CELLS // 2, 256:320], video[CELLS // 2 :, 256:320]], axis=1
    )
    rest = jnp.concatenate([emb[0], jnp.zeros((1, 64), F32)], axis=1)
    rows = []
    for n in range(3):
        part = rest.astype(BF).astype(F32)
        rest = rest - part
        rows += [part[:, 0:128], part[:, 128:256], part[:, 256:384]]
    rows.append(jnp.zeros((7, 128), F32))
    out[pl.ds(PACKED - 16, 16), :] = jnp.concatenate(rows, axis=0).astype(BF)


def line_kernel(pieces, out):
    both = [jnp.concatenate([pieces[zl].astype(F32), pieces[8 + zl].astype(F32)], axis=0) for zl in range(8)]
    pad = jnp.zeros((48, 16), F32)
    groups = [jnp.concatenate([b[:, 30 * a : 30 * a + 30] for b in both] + [pad], axis=1) for a in range(4)]
    block = jnp.concatenate(groups, axis=1).astype(BF)
    for n in range(16):
        out[n] = block


def act_kernel(*refs):
    count = (len(refs) - 8) // 3
    frames = refs[:count]
    gain, shift, same, order, perm_hbm = refs[count : count + 5]
    outs = refs[count + 5 : 3 * count + 5]
    perm, out, sems = refs[3 * count + 5 :]
    move = Mover(sems)
    perm_copy = move.start(perm_hbm, perm)
    chunk = 256
    half = CELLS // 2
    column = lax.rem(lax.broadcasted_iota(jnp.int32, (chunk, 256), 0), COLS)
    low = lax.broadcasted_iota(jnp.int32, (chunk, 128), 1) < 64
    cells = CELLS * C // GROUPS

    def shifted(v):
        edge = column[:, : v.shape[1]]
        before = jnp.where(edge == 0, 0.0, pltpu.roll(v, 1, 0))
        after = jnp.where(edge == COLS - 1, 0.0, pltpu.roll(v, chunk - 1, 0))
        return before, v, after

    copies = []
    for f, frame in enumerate(frames):
        main = lambda i: jnp.concatenate(
            [frame[pl.ds(i * chunk, chunk), :], frame[pl.ds(CELLS + i * chunk, chunk), :]], axis=1
        ).astype(F32)
        rest = lambda i: frame[pl.ds(2 * CELLS + i * chunk, chunk), :].astype(F32)
        s = jnp.zeros((8, 256), F32)
        q = jnp.zeros((8, 256), F32)
        for i in range(CELLS // chunk):
            v = main(i).reshape(chunk // 8, 8, 256)
            s, q = s + jnp.sum(v, axis=0), q + jnp.sum(v * v, axis=0)
        s2 = jnp.zeros((8, 128), F32)
        q2 = jnp.zeros((8, 128), F32)
        for i in range(half // chunk):
            v = rest(i).reshape(chunk // 8, 8, 128)
            s2, q2 = s2 + jnp.sum(v, axis=0), q2 + jnp.sum(v * v, axis=0)
        s = jnp.concatenate([s, s2[:, :64] + s2[:, 64:]], axis=1)
        q = jnp.concatenate([q, q2[:, :64] + q2[:, 64:]], axis=1)
        both = exact(jnp.concatenate([s, q], axis=0), same[...]) / cells
        mean = jnp.sum(both[:8], axis=0, keepdims=True)
        square = jnp.sum(both[8:], axis=0, keepdims=True)
        scale = lax.rsqrt(square - mean * mean + EPS) * gain[...].reshape(1, C)
        offset = shift[...].reshape(1, C) - mean * scale
        scale2 = jnp.concatenate([scale[:, 256:], scale[:, 256:]], axis=1)
        offset2 = jnp.concatenate([offset[:, 256:], offset[:, 256:]], axis=1)
        scale, offset = scale[:, :256], offset[:, :256]
        rows = frame[pl.ds(PACKED - 16, 16), :].astype(F32)
        parts = [
            jnp.concatenate([rows[n : n + 1], rows[n + 1 : n + 2], rows[n + 2 : n + 3, :64]], axis=1) for n in (0, 3, 6)
        ]
        parts = jnp.concatenate(parts + [jnp.zeros((5, C), F32)], axis=0).astype(BF)
        outs[2 * f + 1][...] = jnp.sum(jnp.dot(parts, order[...], preferred_element_type=F32), axis=0, keepdims=True)
        out[f, pl.ds(0, COLS), :] = jnp.zeros((COLS, KPAD), BF)
        out[f, pl.ds(CELLS + COLS, COLS), :] = jnp.zeros((COLS, KPAD), BF)
        if f == 0:
            perm_copy.wait()
        for i in range(half // chunk):
            before2, v2, after2 = shifted(silu(rest(i) * scale2 + offset2).astype(BF).astype(F32))
            swap = lambda v: pltpu.roll(v, 64, 1)
            tails = [
                (jnp.where(low, before2, swap(v2)), jnp.where(low, after2, 0.0)),
                (jnp.where(low, swap(before2), v2), jnp.where(low, swap(after2), 0.0)),
            ]
            for n in range(2):
                at = i + n * (half // chunk)
                taps = shifted(silu(main(at) * scale + offset).astype(BF).astype(F32))
                taps = jnp.concatenate(taps + tails[n], axis=1).astype(BF)
                total = jnp.dot(taps, perm[...], preferred_element_type=F32)
                out[f, pl.ds(at * chunk + COLS, chunk), :] = total.astype(BF)
        copies.append(move.start(out.at[f], outs[2 * f]))
    for copy in copies:
        copy.wait()


def place_weights(half, block, w):
    for y in range(4):
        for x in range(4):
            for a in range(4):
                rows = pl.ds(pl.multiple_of(half + 48 * y, 16), 48)
                w[a, rows, 256 * x : 256 * x + 256] = block[4 * y + x, :, 256 * a : 256 * a + 256]


def convolve(i, cols, w, emb):
    total = jnp.zeros((CPAD, 256), F32)
    for a in range(3):
        total += nt(w[a], cols[pl.ds(i * 256 + COLS * a, 256), :])
    return (total.T + emb).astype(BF)


def own_kernel(cols_hbm, own_hbm, other_hbm, emb, hidden_hbm, stats, w_hbm, cols, own, other, hidden, w, sems):
    move = Mover(sems)
    own_copy = move.start(own_hbm, own)
    other_copy = move.start(other_hbm, other)
    cols_copy = move.start(cols_hbm, cols)
    mine = lax.axis_index("core") * HALF
    own_copy.wait()
    place_weights(mine, own, w)
    other_copy.wait()
    place_weights(HALF - mine, other, w)
    cols_copy.wait()
    copies = [move.start(w, w_hbm)]
    s = jnp.zeros((8, CPAD), F32)
    q = jnp.zeros((8, CPAD), F32)
    for i in range(CELLS // 256):
        h = convolve(i, cols, w, emb[...])
        hidden[pl.ds(i * 256, 256), :] = h
        h = h.astype(F32).reshape(32, 8, CPAD)
        s, q = s + jnp.sum(h, axis=0), q + jnp.sum(h * h, axis=0)
    copies.append(move.start(hidden, hidden_hbm))
    s = jnp.sum(s, axis=0, keepdims=True)
    q = jnp.sum(q, axis=0, keepdims=True)
    rows = [s[:, :128], s[:, 128:256], s[:, 256:], q[:, :128], q[:, 128:256], q[:, 256:], jnp.zeros((2, 128), F32)]
    block = jnp.concatenate(rows, axis=0)
    for n in range(32):
        stats[n] = block
    for copy in copies:
        copy.wait()


def temporal_kernel(w_hbm, perm, order, gain, shift, out, affine, w, sems):
    move = Mover(sems)
    move.start(w_hbm.at[3], w).wait()
    frame = lax.axis_index("zl") * 4 + lax.axis_index("x")
    keep = [(frame > 0).astype(F32), 1.0, (frame < 31).astype(F32)]
    spread = [jnp.dot(w[:, 256 * x : 256 * x + 256], perm[x], preferred_element_type=F32) for x in range(4)]
    left, right = spread[0] + spread[1], spread[2] + spread[3]
    for t in range(3):
        a, b = left[:, 256 * t : 256 * t + 256], right[:, 256 * t : 256 * t + 256]
        part = jnp.concatenate([a[:, :128], a[:, 128:] + b[:, :128], b[:, 128:]], axis=1).astype(BF)
        part = jnp.dot(order[...], part, preferred_element_type=F32) * keep[t]
        out[:, CPAD * t : CPAD * t + CPAD] = part.astype(BF)
    out[:, 3 * CPAD :] = order[...]
    rest = jnp.concatenate([gain[...].reshape(1, C), shift[...].reshape(1, C), jnp.zeros((6, C), F32)], axis=0)
    total = jnp.zeros((8, CPAD), F32)
    for n in range(3):
        part = rest.astype(BF)
        rest = rest - part.astype(F32)
        total += jnp.dot(part, order[...], preferred_element_type=F32)
    affine[...] = total


def final_kernel(
    cols0_hbm, cols2_hbm, w_hbm, hidden_hbm, last_hbm, emb0, emb2, stats, affine, same, bias, out_hbm,
    cols0, cols2, w, hidden, last, out, sems,
):
    move = Mover(sems)
    first, second = pl.ds(0, 640), pl.ds(640, CELLS + 2 * COLS - 640)
    begin = [move.start(w_hbm.at[pl.ds(0, 3)], w)]
    begin += [move.start(h.at[first], c.at[first]) for h, c in ((cols0_hbm, cols0), (cols2_hbm, cols2))]
    later = [move.start(h.at[second], c.at[second]) for h, c in ((cols0_hbm, cols0), (cols2_hbm, cols2))]
    later += [move.start(hidden_hbm, hidden), move.start(last_hbm, last)]
    total = stats[0]
    for n in range(1, 32):
        total = total + stats[n]
    s = jnp.concatenate([total[0:1], total[1:2], total[2:3]], axis=1)
    q = jnp.concatenate([total[3:4], total[4:5], total[5:6]], axis=1)
    both = jnp.concatenate([s, q, jnp.zeros((6, CPAD), F32)], axis=0)
    both = exact(both, same[...]) / (CELLS * 32 * C // GROUPS)
    mean, square = both[0:1], both[1:2]
    scale = lax.rsqrt(square - mean * mean + EPS) * affine[0:1]
    offset = affine[1:2] - mean * scale
    bias_row = bias[...].reshape(1, C)
    mix = lambda h: silu(h.astype(F32) * scale + offset).astype(BF)
    for copy in begin:
        copy.wait()
    near = lambda i: (convolve(i, cols0, w, emb0[...]), convolve(i, cols2, w, emb2[...]))
    ready = [near(0), near(1)]
    for copy in later:
        copy.wait()
    copies = []
    for i in range(CELLS // 256):
        now = ready.pop(0)
        if i < CELLS // 256 - 2:
            ready.append(near(i + 2))
        here = pl.ds(i * 256, 256)
        h = hidden[here, :]
        taps = jnp.concatenate([mix(now[0]), mix(h), mix(now[1]), h], axis=1)
        out[here, :] = (nt(last[...], taps).T + bias_row).astype(BF)
        if i == 2:
            copies.append(move.start(out.at[pl.ds(0, 768)], out_hbm.at[pl.ds(0, 768)]))
    copies.append(move.start(out.at[pl.ds(768, 768)], out_hbm.at[pl.ds(768, 768)]))
    for copy in copies:
        copy.wait()


FILL = 7_500_000_000
FRAME = ("zl", "x")
FORWARD = [(i, i + 1) for i in range(31)]
BACKWARD = [(i + 1, i) for i in range(31)]


def body(video, emb, gain1, shift1, gain2, shift2, sw, tw, bias):
    struct = jax.ShapeDtypeStruct
    const = lambda a, t=BF: jnp.asarray(a, t)
    sems = pltpu.SemaphoreType.DMA
    buffer = lambda *shape: pltpu.VMEM(shape, BF)
    cols = (CELLS + 2 * COLS, KPAD)

    (pieces,) = call(pack_kernel, [struct((16, 24, 128), BF)], "vv")(sw.transpose(0, 2, 1), tw.transpose(1, 0, 2))
    (frame1,) = call(frame_kernel, [struct((PACKED, 128), BF)], "vv")(video.reshape(CELLS, C), emb)
    line = lax.all_to_all(pieces, ("zh", "zl"), 0, 0)
    frame0 = lax.ppermute(frame1, FRAME, FORWARD)
    frame2 = lax.ppermute(frame1, FRAME, BACKWARD)

    act = lambda frames, flops=100_000_000: call(
        act_kernel,
        [struct(cols, BF), struct((1, CPAD), F32)] * len(frames),
        "v" * len(frames) + "vvvva",
        "av" * len(frames),
        [buffer(KPAD, KPAD), buffer(len(frames), *cols), sems((1 + len(frames),))],
        flops,
    )(*frames, gain1, shift1, const(SAME1, F32), const(ORDER), const(ACT_PERM))
    cols1, emb1 = act([frame1])
    (block,) = call(line_kernel, [struct((16, 48, KPAD), BF)], "v")(line)
    own = lax.all_to_all(block, ("y", "x"), 0, 0)
    cols0, emb0, cols2, emb2 = act([frame0, frame2], FILL)
    own, cols0, cols1 = lax.optimization_barrier((own, cols0, cols1))
    other = lax.ppermute(own, "core", [(0, 1), (1, 0)])

    blocks = (16, 48, KPAD)
    hidden1, stats, w = call(
        own_kernel,
        [struct((CELLS, CPAD), BF), struct((32, 8, 128), F32), struct((4, CPAD, KPAD), BF)],
        "aaav",
        "ava",
        [buffer(*cols), buffer(*blocks), buffer(*blocks), buffer(CELLS, CPAD), buffer(4, CPAD, KPAD), sems((5,))],
    )(cols1, own, other, emb1)
    stats = lax.all_to_all(stats, FRAME, 0, 0)
    last, affine = call(
        temporal_kernel,
        [struct((C, 4 * CPAD), BF), struct((8, CPAD), F32)],
        "avvvv",
        scratch=[buffer(CPAD, KPAD), sems((1,))],
        flops=3_000_000_000,
    )(w, const(TEMP_PERM), const(ORDER), gain2, shift2)
    (out,) = call(
        final_kernel,
        [struct((CELLS, C), BF)],
        "aaaaavvvvvv",
        "a",
        [
            buffer(*cols),
            buffer(*cols),
            buffer(3, CPAD, KPAD),
            buffer(CELLS, CPAD),
            buffer(C, 4 * CPAD),
            buffer(CELLS, C),
            sems((9,)),
        ],
    )(cols0, cols2, w, hidden1, last, emb0, emb2, stats, affine, const(SAME2, F32), bias)
    return out.reshape(video.shape)


def solution(mesh):
    split = Mesh(mesh.devices.reshape(4, 2, 2, 8, 4), ("y", "zh", "core", "zl", "x"))
    dp = ("y", "zh", "core")
    data = P(dp, FRAME, None, None, None)
    placed = (data, P(dp, FRAME, None), P(), P(), P(), P(), P(None, FRAME, dp), P(None, FRAME, dp), P())
    return jax.shard_map(body, mesh=split, in_specs=placed, out_specs=data, check_vma=False)
```

```python
import functools

import jax
import jax.numpy as jnp
import numpy as np
from jax import lax
from jax.experimental import pallas as pl
from jax.experimental.pallas import tpu as pltpu
from jax.sharding import Mesh, PartitionSpec as P

GROUPS = 32
C = 320
CELLS = 1536
COLS = 64
EPS = 1e-5
BF = jnp.bfloat16
F32 = jnp.float32
KPAD = 1024
CPAD = 384
HALF = 192
PACKED = CELLS * 5 // 2
VMEM = 60 * 1024 * 1024


def _consts():
    act_perm = np.zeros((KPAD, KPAD), np.float32)
    for f in range(32):
        zl, x = divmod(f, 4)
        for kk in range(30):
            b, i = divmod(30 * f + kk, C)
            row = 256 * b + i if i < 256 else 768 + 64 * b + i - 256
            act_perm[row, 256 * x + 30 * zl + kk] = 1
    chan = np.zeros(C, np.int64)
    for i in range(C):
        d, j = divmod(i, 20)
        y, zh, core = d // 4, (d // 2) % 2, d % 2
        chan[i] = HALF * core + 48 * y + 24 * zh + j
    order = np.zeros((C, CPAD), np.float32)
    order[np.arange(C), chan] = 1
    temp_perm = np.zeros((KPAD, KPAD), np.float32)
    for x in range(4):
        for t in range(3):
            for zl in range(8):
                for kk in range(10):
                    i = 40 * zl + 10 * x + kk
                    to = 256 * t + i if i < 256 else 768 + 64 * t + i - 256
                    temp_perm[256 * x + 30 * zl + 10 * t + kk, to] = 1
    same1 = np.kron(np.eye(GROUPS), np.ones((10, 10))).astype(np.float32)
    return act_perm, order, temp_perm, same1


ACT_PERM, ORDER, TEMP_PERM, SAME1 = _consts()


def call(kernel, out_shape, ins, outs=None, scratch=(), flops=0, vmem=VMEM):
    space = {"v": pltpu.VMEM, "a": pl.ANY}
    specs = lambda letters: [pl.BlockSpec(memory_space=space[c]) for c in letters]
    outs = specs(outs or "v" * len(out_shape))
    return pl.pallas_call(
        kernel,
        out_shape=tuple(out_shape),
        in_specs=specs(ins),
        out_specs=tuple(outs),
        scratch_shapes=list(scratch),
        compiler_params=pltpu.CompilerParams(vmem_limit_bytes=vmem),
        cost_estimate=pl.CostEstimate(flops=flops, bytes_accessed=0, transcendentals=0),
    )


class Mover:
    def __init__(self, sems):
        self.sems, self.used = sems, 0

    def start(self, src, dst):
        copy = pltpu.make_async_copy(src, dst, self.sems.at[self.used])
        self.used += 1
        copy.start()
        return copy


def exact(a, b):
    return jnp.dot(a, b, precision=lax.Precision.HIGHEST, preferred_element_type=F32)


def nt(a, b):
    return lax.dot_general(a, b, (((1,), (1,)), ((), ())), preferred_element_type=F32)


def silu(v):
    half = 0.5 * v
    return half + half * jnp.tanh(half)


def pack_kernel(sw, tw, out):
    lane = lax.broadcasted_iota(jnp.int32, (30, 128), 1)
    row = lax.broadcasted_iota(jnp.int32, (30, 128), 0)
    total = jnp.zeros((20, 128), F32)
    for a in range(3):
        total += jnp.dot(sw[a], (lane == row + 30 * a).astype(F32).astype(BF), preferred_element_type=F32)
    rows = jnp.concatenate([tw[r].astype(F32) for r in range(10)], axis=0).astype(BF)
    spread = (lane == 90 + 10 * lax.rem(row, 3) + lax.div(row, 3)).astype(F32).astype(BF)
    total += lax.dot_general(rows, spread, (((0,), (0,)), ((), ())), preferred_element_type=F32)
    piece = jnp.concatenate([total, jnp.zeros((4, 128), F32)], axis=0).astype(BF)
    for n in range(16):
        out[n] = piece


def line_kernel(pieces, out):
    both = [jnp.concatenate([pieces[zl].astype(F32), pieces[8 + zl].astype(F32)], axis=0) for zl in range(8)]
    pad = jnp.zeros((48, 16), F32)
    groups = [jnp.concatenate([b[:, 30 * a : 30 * a + 30] for b in both] + [pad], axis=1) for a in range(4)]
    block = jnp.concatenate(groups, axis=1).astype(BF)
    for n in range(16):
        out[n] = block


def pair(v):
    return v[:, :64] + v[:, 64:]


def moments(chunks):
    s = q = 0.0
    for v in chunks:
        v = v.reshape(-1, 8, v.shape[1])
        s, q = s + jnp.sum(v, axis=0), q + jnp.sum(v * v, axis=0)
    return s, q


def act_kernel(video, gain, shift, same, perm_hbm, out_hbm, perm, out, sems):
    move = Mover(sems)
    perm_copy = move.start(perm_hbm, perm)
    chunk = 256
    column = lax.rem(lax.broadcasted_iota(jnp.int32, (chunk, 256), 0), COLS)
    low = lax.broadcasted_iota(jnp.int32, (chunk, 128), 1) < 64

    def shifted(v):
        edge = column[:, : v.shape[1]]
        before = jnp.where(edge == 0, 0.0, pltpu.roll(v, 1, 0))
        after = jnp.where(edge == COLS - 1, 0.0, pltpu.roll(v, chunk - 1, 0))
        return before, v, after

    main = lambda i: video[pl.ds(i * chunk, chunk), 0:256].astype(F32)
    tail = lambda i: video[pl.ds(i * chunk, chunk), 256:320].astype(F32)
    rest = lambda i: jnp.concatenate([tail(i), tail(i + 3)], axis=1)
    s, q = moments(main(i) for i in range(6))
    s2, q2 = moments(rest(i) for i in range(3))
    s = jnp.concatenate([s, pair(s2)], axis=1)
    q = jnp.concatenate([q, pair(q2)], axis=1)
    both = exact(jnp.concatenate([s, q], axis=0), same[...]) / (CELLS * C // GROUPS)
    mean = jnp.sum(both[:8], axis=0, keepdims=True)
    square = jnp.sum(both[8:], axis=0, keepdims=True)
    scale = lax.rsqrt(square - mean * mean + EPS) * gain[...].reshape(1, C)
    offset = shift[...].reshape(1, C) - mean * scale
    scale2 = jnp.concatenate([scale[:, 256:], scale[:, 256:]], axis=1)
    offset2 = jnp.concatenate([offset[:, 256:], offset[:, 256:]], axis=1)
    scale, offset = scale[:, :256], offset[:, :256]
    out[pl.ds(0, COLS), :] = jnp.zeros((COLS, KPAD), BF)
    out[pl.ds(CELLS + COLS, COLS), :] = jnp.zeros((COLS, KPAD), BF)
    perm_copy.wait()
    swap = lambda v: pltpu.roll(v, 64, 1)
    for i in range(3):
        before2, v2, after2 = shifted(silu(rest(i) * scale2 + offset2).astype(BF).astype(F32))
        tails = [
            (jnp.where(low, before2, swap(v2)), jnp.where(low, after2, 0.0)),
            (jnp.where(low, swap(before2), v2), jnp.where(low, swap(after2), 0.0)),
        ]
        for n in range(2):
            at = i + 3 * n
            taps = shifted(silu(main(at) * scale + offset).astype(BF).astype(F32))
            taps = jnp.concatenate(taps + tails[n], axis=1).astype(BF)
            total = jnp.dot(taps, perm[...], preferred_element_type=F32)
            out[pl.ds(at * chunk + COLS, chunk), :] = total.astype(BF)
    move.start(out, out_hbm).wait()


def place_weights(half, block, w):
    for y in range(4):
        for x in range(4):
            for a in range(4):
                rows = pl.ds(pl.multiple_of(half + 48 * y, 16), 48)
                w[a, rows, 256 * x : 256 * x + 256] = block[4 * y + x, :, 256 * a : 256 * a + 256]


def own_kernel(cols_hbm, own_hbm, other_hbm, emb, order, hidden_hbm, stats, last_hbm, cols, own, other, hidden, w, natural, sems):
    move = Mover(sems)
    own_copy = move.start(own_hbm, own)
    other_copy = move.start(other_hbm, other)
    cols_copy = move.start(cols_hbm, cols)
    mine = lax.axis_index("core") * HALF
    own_copy.wait()
    place_weights(mine, own, w)
    other_copy.wait()
    place_weights(HALF - mine, other, w)
    cols_copy.wait()
    for a in range(4):
        natural[a] = jnp.dot(order[...], w[a], preferred_element_type=F32).astype(BF)
    s = q = jnp.zeros((8, C), F32)
    for i in (0, 3, 1, 4, 2, 5):
        total = jnp.zeros((C, 256), F32)
        for a in range(3):
            total += nt(natural[a], cols[pl.ds(i * 256 + COLS * a, 256), :])
        h = (total.T + emb[0]).astype(BF)
        hidden[pl.ds(i * 256, 256), :] = h[:, :128]
        hidden[pl.ds(CELLS + i * 256, 256), :] = h[:, 128:256]
        h = h.astype(F32)
        if i < 3:
            rest = h[:, 256:]
        else:
            both = jnp.concatenate([rest, h[:, 256:]], axis=1)
            hidden[pl.ds(2 * CELLS + (i - 3) * 256, 256), :] = both.astype(BF)
        h = h.reshape(32, 8, C)
        s, q = s + jnp.sum(h, axis=0), q + jnp.sum(h * h, axis=0)
    copies = [move.start(hidden, hidden_hbm), move.start(natural.at[3], last_hbm)]
    s = jnp.sum(s, axis=0, keepdims=True)
    q = jnp.sum(q, axis=0, keepdims=True)
    tail = jnp.concatenate([s[:, 256:], q[:, 256:]], axis=1)
    rows = [s[:, :128], s[:, 128:256], q[:, :128], q[:, 128:256], tail, jnp.zeros((3, 128), F32)]
    block = jnp.concatenate(rows, axis=0)
    for n in range(32):
        stats[n] = block
    for copy in copies:
        copy.wait()


def temporal_kernel(w, perm, out):
    frame = lax.axis_index("zl") * 4 + lax.axis_index("x")
    lane = lax.broadcasted_iota(jnp.int32, (1, KPAD), 1)
    tap = jnp.where(lane < 768, lane // 256, (lane - 768) // 64)
    keep = jnp.where(tap == 0, (frame > 0).astype(F32), jnp.where(tap == 2, (frame < 31).astype(F32), 1.0))
    out[...] = (jnp.dot(w[...], perm[...], preferred_element_type=F32) * keep).astype(BF)


def final_kernel(hidden0, hidden1, hidden2, stats, gain, shift, same, bias, last, out):
    total = stats[0]
    for n in range(1, 32):
        total = total + stats[n]
    s = jnp.concatenate([total[0:1], total[1:2], total[4:5, :64]], axis=1)
    q = jnp.concatenate([total[2:3], total[3:4], total[4:5, 64:]], axis=1)
    both = jnp.concatenate([s, q, jnp.zeros((6, C), F32)], axis=0)
    both = exact(both, same[...]) / (CELLS * 32 * C // GROUPS)
    mean, square = both[0:1], both[1:2]
    scale = lax.rsqrt(square - mean * mean + EPS) * gain[...].reshape(1, C)
    offset = shift[...].reshape(1, C) - mean * scale
    tiles = [(scale[:, n : n + 128], offset[:, n : n + 128]) for n in (0, 128)]
    tiles.append(tuple(jnp.concatenate([v[:, 256:], v[:, 256:]], axis=1) for v in (scale, offset)))
    bias_row = bias[...].reshape(1, C)
    low = lax.broadcasted_iota(jnp.int32, (256, 128), 1) < 64
    swap = lambda v: pltpu.roll(v, 64, 1)
    frames = (hidden0, hidden1, hidden2)

    def mix(h, start, tile):
        v = h[pl.ds(start, 256), :].astype(F32)
        return silu(v * tiles[tile][0] + tiles[tile][1])

    for i in range(3):
        a, b, c = (mix(h, 2 * CELLS + i * 256, 2) for h in frames)
        tails = [
            (jnp.where(low, a, swap(b)), jnp.where(low, c, 0.0)),
            (jnp.where(low, swap(a), b), jnp.where(low, swap(c), 0.0)),
        ]
        rest = hidden1[pl.ds(2 * CELLS + i * 256, 256), :].astype(F32)
        for n in range(2):
            at = i + 3 * n
            parts = [mix(h, tile * CELLS + at * 256, tile) for h in frames for tile in range(2)]
            taps = jnp.concatenate(parts + list(tails[n]), axis=1).astype(BF)
            moved = (nt(last[...], taps).T + bias_row).astype(BF).astype(F32)
            here = pl.ds(at * 256, 256)
            h = [hidden1[pl.ds(tile * CELLS + at * 256, 256), :].astype(F32) for tile in range(2)]
            h.append(rest[:, :64] if n == 0 else rest[:, 64:])
            out[here, :] = (moved + jnp.concatenate(h, axis=1)).astype(BF)


FILL = 5_000_000_000
FRAME = ("zl", "x")
FORWARD = [(i, i + 1) for i in range(31)]
BACKWARD = [(i + 1, i) for i in range(31)]


def body(video, emb, gain1, shift1, gain2, shift2, sw, tw, bias):
    struct = jax.ShapeDtypeStruct
    const = lambda a, t=BF: jnp.asarray(a, t)
    sems = pltpu.SemaphoreType.DMA
    buffer = lambda *shape: pltpu.VMEM(shape, BF)
    cols = (CELLS + 2 * COLS, KPAD)
    blocks = (16, 48, KPAD)

    (pieces,) = call(pack_kernel, [struct((16, 24, 128), BF)], "vv")(sw.transpose(0, 2, 1), tw.transpose(1, 0, 2))
    line = lax.all_to_all(pieces, ("zh", "zl"), 0, 0)
    (block,) = call(line_kernel, [struct(blocks, BF)], "v")(line)
    own = lax.all_to_all(block, ("y", "x"), 0, 0)
    (cols1,) = call(
        act_kernel,
        [struct(cols, BF)],
        "vvvva",
        "a",
        [buffer(KPAD, KPAD), buffer(*cols), sems((2,))],
        FILL,
    )(video.reshape(CELLS, C), gain1, shift1, const(SAME1, F32), const(ACT_PERM))
    own, cols1 = lax.optimization_barrier((own, cols1))
    other = lax.ppermute(own, "core", [(0, 1), (1, 0)])

    hidden1, stats, w = call(
        own_kernel,
        [struct((PACKED, 128), BF), struct((32, 8, 128), F32), struct((C, KPAD), BF)],
        "aaavv",
        "ava",
        [
            buffer(*cols),
            buffer(*blocks),
            buffer(*blocks),
            buffer(PACKED, 128),
            buffer(4, CPAD, KPAD),
            buffer(4, C, KPAD),
            sems((5,)),
        ],
    )(cols1, own, other, emb, const(ORDER))
    hidden0 = lax.ppermute(hidden1, FRAME, FORWARD)
    hidden2 = lax.ppermute(hidden1, FRAME, BACKWARD)
    stats = lax.all_to_all(stats, FRAME, 0, 0)
    (last,) = call(temporal_kernel, [struct((C, KPAD), BF)], "vv", flops=5_000_000_000)(w, const(TEMP_PERM))
    (out,) = call(final_kernel, [struct((CELLS, C), BF)], "v" * 9)(
        hidden0, hidden1, hidden2, stats, gain2, shift2, const(SAME1, F32), bias, last
    )
    return out.reshape(video.shape)


def solution(mesh):
    split = Mesh(mesh.devices.reshape(4, 2, 2, 8, 4), ("y", "zh", "core", "zl", "x"))
    dp = ("y", "zh", "core")
    data = P(dp, FRAME, None, None, None)
    placed = (data, P(dp, FRAME, None), P(), P(), P(), P(), P(None, FRAME, dp), P(None, FRAME, dp), P())
    return jax.shard_map(body, mesh=split, in_specs=placed, out_specs=data, check_vma=False)
```

```python
import functools

import jax
import jax.numpy as jnp
import numpy as np
from jax import lax
from jax.experimental import pallas as pl
from jax.experimental.pallas import tpu as pltpu
from jax.sharding import Mesh, PartitionSpec as P

GROUPS = 32
C = 320
CELLS = 1536
COLS = 64
EPS = 1e-5
BF = jnp.bfloat16
F32 = jnp.float32
KPAD = 1024
CPAD = 384
HALF = 192
PACKED = CELLS * 5 // 2
FIRST = 1792
VMEM = 60 * 1024 * 1024


def _consts():
    act_perm = np.zeros((KPAD, KPAD), np.float32)
    for f in range(32):
        zl, x = divmod(f, 4)
        for kk in range(30):
            b, i = divmod(30 * f + kk, C)
            row = 256 * b + i if i < 256 else 768 + 64 * b + i - 256
            act_perm[row, 256 * x + 30 * zl + kk] = 1
    chan = np.zeros(C, np.int64)
    for i in range(C):
        d, j = divmod(i, 20)
        y, zh, core = d // 4, (d // 2) % 2, d % 2
        chan[i] = HALF * core + 48 * y + 24 * zh + j
    order = np.zeros((C, CPAD), np.float32)
    order[np.arange(C), chan] = 1
    temp_perm = np.zeros((KPAD, KPAD), np.float32)
    for x in range(4):
        for t in range(3):
            for zl in range(8):
                for kk in range(10):
                    i = 40 * zl + 10 * x + kk
                    to = 256 * t + i if i < 256 else 768 + 64 * t + i - 256
                    temp_perm[256 * x + 30 * zl + 10 * t + kk, to] = 1
    same1 = np.kron(np.eye(GROUPS), np.ones((10, 10))).astype(np.float32)
    return act_perm, order, temp_perm, same1


ACT_PERM, ORDER, TEMP_PERM, SAME1 = _consts()


def call(kernel, out_shape, ins, outs=None, scratch=(), flops=0, vmem=VMEM):
    space = {"v": pltpu.VMEM, "a": pl.ANY}
    specs = lambda letters: [pl.BlockSpec(memory_space=space[c]) for c in letters]
    outs = specs(outs or "v" * len(out_shape))
    return pl.pallas_call(
        kernel,
        out_shape=tuple(out_shape),
        in_specs=specs(ins),
        out_specs=tuple(outs),
        scratch_shapes=list(scratch),
        compiler_params=pltpu.CompilerParams(vmem_limit_bytes=vmem),
        cost_estimate=pl.CostEstimate(flops=flops, bytes_accessed=0, transcendentals=0),
    )


class Mover:
    def __init__(self, sems):
        self.sems, self.used = sems, 0

    def start(self, src, dst):
        copy = pltpu.make_async_copy(src, dst, self.sems.at[self.used])
        self.used += 1
        copy.start()
        return copy


def exact(a, b):
    return jnp.dot(a, b, precision=lax.Precision.HIGHEST, preferred_element_type=F32)


def nt(a, b):
    return lax.dot_general(a, b, (((1,), (1,)), ((), ())), preferred_element_type=F32)


def silu(v):
    half = 0.5 * v
    return half + half * jnp.tanh(half)


def pack_kernel(sw, tw, out):
    lane = lax.broadcasted_iota(jnp.int32, (30, 128), 1)
    row = lax.broadcasted_iota(jnp.int32, (30, 128), 0)
    total = jnp.zeros((20, 128), F32)
    for a in range(3):
        total += jnp.dot(sw[a], (lane == row + 30 * a).astype(F32).astype(BF), preferred_element_type=F32)
    rows = jnp.concatenate([tw[r].astype(F32) for r in range(10)], axis=0).astype(BF)
    spread = (lane == 90 + 10 * lax.rem(row, 3) + lax.div(row, 3)).astype(F32).astype(BF)
    total += lax.dot_general(rows, spread, (((0,), (0,)), ((), ())), preferred_element_type=F32)
    piece = jnp.concatenate([total, jnp.zeros((4, 128), F32)], axis=0).astype(BF)
    for n in range(16):
        out[n] = piece


def line_kernel(pieces, out):
    both = [jnp.concatenate([pieces[zl].astype(F32), pieces[8 + zl].astype(F32)], axis=0) for zl in range(8)]
    pad = jnp.zeros((48, 16), F32)
    groups = [jnp.concatenate([b[:, 30 * a : 30 * a + 30] for b in both] + [pad], axis=1) for a in range(4)]
    block = jnp.concatenate(groups, axis=1).astype(BF)
    for n in range(16):
        out[n] = block


def pair(v):
    return v[:, :64] + v[:, 64:]


def moments(chunks):
    s = q = 0.0
    for v in chunks:
        v = v.reshape(-1, 8, v.shape[1])
        s, q = s + jnp.sum(v, axis=0), q + jnp.sum(v * v, axis=0)
    return s, q


def act_kernel(video, gain, shift, same, perm_hbm, out_hbm, perm, out, sems):
    move = Mover(sems)
    perm_copy = move.start(perm_hbm, perm)
    chunk = 256
    column = lax.rem(lax.broadcasted_iota(jnp.int32, (chunk, 256), 0), COLS)
    low = lax.broadcasted_iota(jnp.int32, (chunk, 128), 1) < 64

    def shifted(v):
        edge = column[:, : v.shape[1]]
        before = jnp.where(edge == 0, 0.0, pltpu.roll(v, 1, 0))
        after = jnp.where(edge == COLS - 1, 0.0, pltpu.roll(v, chunk - 1, 0))
        return before, v, after

    main = lambda i: video[pl.ds(i * chunk, chunk), 0:256].astype(F32)
    tail = lambda i: video[pl.ds(i * chunk, chunk), 256:320].astype(F32)
    rest = lambda i: jnp.concatenate([tail(i), tail(i + 3)], axis=1)
    s, q = moments(main(i) for i in range(6))
    s2, q2 = moments(rest(i) for i in range(3))
    s = jnp.concatenate([s, pair(s2)], axis=1)
    q = jnp.concatenate([q, pair(q2)], axis=1)
    both = exact(jnp.concatenate([s, q], axis=0), same[...]) / (CELLS * C // GROUPS)
    mean = jnp.sum(both[:8], axis=0, keepdims=True)
    square = jnp.sum(both[8:], axis=0, keepdims=True)
    scale = lax.rsqrt(square - mean * mean + EPS) * gain[...].reshape(1, C)
    offset = shift[...].reshape(1, C) - mean * scale
    scale2 = jnp.concatenate([scale[:, 256:], scale[:, 256:]], axis=1)
    offset2 = jnp.concatenate([offset[:, 256:], offset[:, 256:]], axis=1)
    scale, offset = scale[:, :256], offset[:, :256]
    out[pl.ds(0, COLS), :] = jnp.zeros((COLS, KPAD), BF)
    out[pl.ds(CELLS + COLS, COLS), :] = jnp.zeros((COLS, KPAD), BF)
    perm_copy.wait()
    swap = lambda v: pltpu.roll(v, 64, 1)
    for i in range(3):
        before2, v2, after2 = shifted(silu(rest(i) * scale2 + offset2).astype(BF).astype(F32))
        tails = [
            (jnp.where(low, before2, swap(v2)), jnp.where(low, after2, 0.0)),
            (jnp.where(low, swap(before2), v2), jnp.where(low, swap(after2), 0.0)),
        ]
        for n in range(2):
            at = i + 3 * n
            taps = shifted(silu(main(at) * scale + offset).astype(BF).astype(F32))
            taps = jnp.concatenate(taps + tails[n], axis=1).astype(BF)
            total = jnp.dot(taps, perm[...], preferred_element_type=F32)
            out[pl.ds(at * chunk + COLS, chunk), :] = total.astype(BF)
    move.start(out, out_hbm).wait()


def place_weights(half, block, w):
    for y in range(4):
        for x in range(4):
            for a in range(4):
                rows = pl.ds(pl.multiple_of(half + 48 * y, 16), 48)
                w[a, rows, 256 * x : 256 * x + 256] = block[4 * y + x, :, 256 * a : 256 * a + 256]


def own_kernel(cols_hbm, own_hbm, other_hbm, emb, order, first_hbm, second_hbm, stats, last_hbm, cols, own, other, hidden, w, natural, sems):
    move = Mover(sems)
    own_copy = move.start(own_hbm, own)
    other_copy = move.start(other_hbm, other)
    cols_copy = move.start(cols_hbm, cols)
    mine = lax.axis_index("core") * HALF
    own_copy.wait()
    place_weights(mine, own, w)
    other_copy.wait()
    place_weights(HALF - mine, other, w)
    cols_copy.wait()
    for a in range(4):
        natural[a] = jnp.dot(order[...], w[a], preferred_element_type=F32).astype(BF)
    s = q = jnp.zeros((8, C), F32)
    for i in (0, 3, 1, 4, 2, 5):
        total = jnp.zeros((C, 256), F32)
        for a in range(3):
            total += nt(natural[a], cols[pl.ds(i * 256 + COLS * a, 256), :])
        h = (total.T + emb[0]).astype(BF)
        hidden[pl.ds(i * 256, 256), :] = h[:, :128]
        hidden[pl.ds(CELLS + i * 256, 256), :] = h[:, 128:256]
        h = h.astype(F32)
        if i < 3:
            rest = h[:, 256:]
        else:
            both = jnp.concatenate([rest, h[:, 256:]], axis=1)
            hidden[pl.ds(2 * CELLS + (i - 3) * 256, 256), :] = both.astype(BF)
        h = h.reshape(32, 8, C)
        s, q = s + jnp.sum(h, axis=0), q + jnp.sum(h * h, axis=0)
    copies = [move.start(hidden.at[pl.ds(0, FIRST)], first_hbm), move.start(hidden.at[pl.ds(FIRST, PACKED - FIRST)], second_hbm)]
    copies.append(move.start(natural.at[3], last_hbm))
    s = jnp.sum(s, axis=0, keepdims=True)
    q = jnp.sum(q, axis=0, keepdims=True)
    tail = jnp.concatenate([s[:, 256:], q[:, 256:]], axis=1)
    rows = [s[:, :128], s[:, 128:256], q[:, :128], q[:, 128:256], tail, jnp.zeros((3, 128), F32)]
    block = jnp.concatenate(rows, axis=0)
    for n in range(32):
        stats[n] = block
    for copy in copies:
        copy.wait()


def temporal_kernel(w, perm, out):
    frame = lax.axis_index("zl") * 4 + lax.axis_index("x")
    lane = lax.broadcasted_iota(jnp.int32, (1, KPAD), 1)
    tap = jnp.where(lane < 768, lane // 256, (lane - 768) // 64)
    keep = jnp.where(tap == 0, (frame > 0).astype(F32), jnp.where(tap == 2, (frame < 31).astype(F32), 1.0))
    out[...] = (jnp.dot(w[...], perm[...], preferred_element_type=F32) * keep).astype(BF)


def final_kernel(first0, second0, first1, second1, first2, second2, stats, gain, shift, same, bias, last, out):
    def rows(frame, start):
        first, second = frame
        ref, at = (first, start) if start < FIRST else (second, start - FIRST)
        return ref[pl.ds(at, 256), :].astype(F32)

    total = stats[0]
    for n in range(1, 32):
        total = total + stats[n]
    s = jnp.concatenate([total[0:1], total[1:2], total[4:5, :64]], axis=1)
    q = jnp.concatenate([total[2:3], total[3:4], total[4:5, 64:]], axis=1)
    both = jnp.concatenate([s, q, jnp.zeros((6, C), F32)], axis=0)
    both = exact(both, same[...]) / (CELLS * 32 * C // GROUPS)
    mean, square = both[0:1], both[1:2]
    scale = lax.rsqrt(square - mean * mean + EPS) * gain[...].reshape(1, C)
    offset = shift[...].reshape(1, C) - mean * scale
    tiles = [(scale[:, n : n + 128], offset[:, n : n + 128]) for n in (0, 128)]
    tiles.append(tuple(jnp.concatenate([v[:, 256:], v[:, 256:]], axis=1) for v in (scale, offset)))
    bias_row = bias[...].reshape(1, C)
    low = lax.broadcasted_iota(jnp.int32, (256, 128), 1) < 64
    swap = lambda v: pltpu.roll(v, 64, 1)
    frames = ((first0, second0), (first1, second1), (first2, second2))

    def mix(h, start, tile):
        v = rows(h, start)
        return silu(v * tiles[tile][0] + tiles[tile][1])

    for i in range(3):
        a, b, c = (mix(h, 2 * CELLS + i * 256, 2) for h in frames)
        tails = [
            (jnp.where(low, a, swap(b)), jnp.where(low, c, 0.0)),
            (jnp.where(low, swap(a), b), jnp.where(low, swap(c), 0.0)),
        ]
        rest = rows(frames[1], 2 * CELLS + i * 256)
        for n in range(2):
            at = i + 3 * n
            parts = [mix(h, tile * CELLS + at * 256, tile) for h in frames for tile in range(2)]
            taps = jnp.concatenate(parts + list(tails[n]), axis=1).astype(BF)
            moved = (nt(last[...], taps).T + bias_row).astype(BF).astype(F32)
            here = pl.ds(at * 256, 256)
            h = [rows(frames[1], tile * CELLS + at * 256) for tile in range(2)]
            h.append(rest[:, :64] if n == 0 else rest[:, 64:])
            out[here, :] = (moved + jnp.concatenate(h, axis=1)).astype(BF)


FILL = 5_000_000_000
FRAME = ("zl", "x")
FORWARD = [(i, i + 1) for i in range(31)]
BACKWARD = [(i + 1, i) for i in range(31)]


def body(video, emb, gain1, shift1, gain2, shift2, sw, tw, bias):
    struct = jax.ShapeDtypeStruct
    const = lambda a, t=BF: jnp.asarray(a, t)
    sems = pltpu.SemaphoreType.DMA
    buffer = lambda *shape: pltpu.VMEM(shape, BF)
    cols = (CELLS + 2 * COLS, KPAD)
    blocks = (16, 48, KPAD)

    (pieces,) = call(pack_kernel, [struct((16, 24, 128), BF)], "vv")(sw.transpose(0, 2, 1), tw.transpose(1, 0, 2))
    line = lax.all_to_all(pieces, ("zh", "zl"), 0, 0)
    (block,) = call(line_kernel, [struct(blocks, BF)], "v")(line)
    own = lax.all_to_all(block, ("y", "x"), 0, 0)
    (cols1,) = call(
        act_kernel,
        [struct(cols, BF)],
        "vvvva",
        "a",
        [buffer(KPAD, KPAD), buffer(*cols), sems((2,))],
        FILL,
    )(video.reshape(CELLS, C), gain1, shift1, const(SAME1, F32), const(ACT_PERM))
    own, cols1 = lax.optimization_barrier((own, cols1))
    other = lax.ppermute(own, "core", [(0, 1), (1, 0)])

    first1, second1, stats, w = call(
        own_kernel,
        [
            struct((FIRST, 128), BF),
            struct((PACKED - FIRST, 128), BF),
            struct((32, 8, 128), F32),
            struct((C, KPAD), BF),
        ],
        "aaavv",
        "aava",
        [
            buffer(*cols),
            buffer(*blocks),
            buffer(*blocks),
            buffer(PACKED, 128),
            buffer(4, CPAD, KPAD),
            buffer(4, C, KPAD),
            sems((6,)),
        ],
    )(cols1, own, other, emb, const(ORDER))
    first0 = lax.ppermute(first1, FRAME, FORWARD)
    first2 = lax.ppermute(first1, FRAME, BACKWARD)
    stats = lax.all_to_all(stats, FRAME, 0, 0)
    second0 = lax.ppermute(second1, FRAME, FORWARD)
    second2 = lax.ppermute(second1, FRAME, BACKWARD)
    (last,) = call(temporal_kernel, [struct((C, KPAD), BF)], "vv", flops=5_000_000_000)(w, const(TEMP_PERM))
    (out,) = call(final_kernel, [struct((CELLS, C), BF)], "v" * 12)(
        first0, second0, first1, second1, first2, second2, stats, gain2, shift2, const(SAME1, F32), bias, last
    )
    return out.reshape(video.shape)


def solution(mesh):
    split = Mesh(mesh.devices.reshape(4, 2, 2, 8, 4), ("y", "zh", "core", "zl", "x"))
    dp = ("y", "zh", "core")
    data = P(dp, FRAME, None, None, None)
    placed = (data, P(dp, FRAME, None), P(), P(), P(), P(), P(None, FRAME, dp), P(None, FRAME, dp), P())
    return jax.shard_map(body, mesh=split, in_specs=placed, out_specs=data, check_vma=False)
```

```python
import functools

import jax
import jax.numpy as jnp
import numpy as np
from jax import lax
from jax.experimental import pallas as pl
from jax.experimental.pallas import tpu as pltpu
from jax.sharding import Mesh, PartitionSpec as P

GROUPS = 32
C = 320
CELLS = 1536
COLS = 64
EPS = 1e-5
BF = jnp.bfloat16
F32 = jnp.float32
KPAD = 1024
CPAD = 384
HALF = 192
PACKED = CELLS * 5 // 2
FIRST = 1024
VMEM = 60 * 1024 * 1024


def _consts():
    act_perm = np.zeros((KPAD, KPAD), np.float32)
    for f in range(32):
        zl, x = divmod(f, 4)
        for kk in range(30):
            b, i = divmod(30 * f + kk, C)
            row = 256 * b + i if i < 256 else 768 + 64 * b + i - 256
            act_perm[row, 256 * x + 30 * zl + kk] = 1
    chan = np.zeros(C, np.int64)
    for i in range(C):
        d, j = divmod(i, 20)
        y, zh, core = d // 4, (d // 2) % 2, d % 2
        chan[i] = HALF * core + 48 * y + 24 * zh + j
    order = np.zeros((C, CPAD), np.float32)
    order[np.arange(C), chan] = 1
    temp_perm = np.zeros((KPAD, KPAD), np.float32)
    for x in range(4):
        for t in range(3):
            for zl in range(8):
                for kk in range(10):
                    i = 40 * zl + 10 * x + kk
                    to = 256 * t + i if i < 256 else 768 + 64 * t + i - 256
                    temp_perm[256 * x + 30 * zl + 10 * t + kk, to] = 1
    same1 = np.kron(np.eye(GROUPS), np.ones((10, 10))).astype(np.float32)
    return act_perm, order, temp_perm, same1


ACT_PERM, ORDER, TEMP_PERM, SAME1 = _consts()


def call(kernel, out_shape, ins, outs=None, scratch=(), flops=0, vmem=VMEM):
    space = {"v": pltpu.VMEM, "a": pl.ANY}
    specs = lambda letters: [pl.BlockSpec(memory_space=space[c]) for c in letters]
    outs = specs(outs or "v" * len(out_shape))
    return pl.pallas_call(
        kernel,
        out_shape=tuple(out_shape),
        in_specs=specs(ins),
        out_specs=tuple(outs),
        scratch_shapes=list(scratch),
        compiler_params=pltpu.CompilerParams(vmem_limit_bytes=vmem),
        cost_estimate=pl.CostEstimate(flops=flops, bytes_accessed=0, transcendentals=0),
    )


class Mover:
    def __init__(self, sems):
        self.sems, self.used = sems, 0

    def start(self, src, dst):
        copy = pltpu.make_async_copy(src, dst, self.sems.at[self.used])
        self.used += 1
        copy.start()
        return copy


def exact(a, b):
    return jnp.dot(a, b, precision=lax.Precision.HIGHEST, preferred_element_type=F32)


def nt(a, b):
    return lax.dot_general(a, b, (((1,), (1,)), ((), ())), preferred_element_type=F32)


def silu(v):
    half = 0.5 * v
    return half + half * jnp.tanh(half)


def pack_kernel(sw, tw, out):
    lane = lax.broadcasted_iota(jnp.int32, (30, 128), 1)
    row = lax.broadcasted_iota(jnp.int32, (30, 128), 0)
    total = jnp.zeros((20, 128), F32)
    for a in range(3):
        total += jnp.dot(sw[a], (lane == row + 30 * a).astype(F32).astype(BF), preferred_element_type=F32)
    rows = jnp.concatenate([tw[r].astype(F32) for r in range(10)], axis=0).astype(BF)
    spread = (lane == 90 + 10 * lax.rem(row, 3) + lax.div(row, 3)).astype(F32).astype(BF)
    total += lax.dot_general(rows, spread, (((0,), (0,)), ((), ())), preferred_element_type=F32)
    piece = jnp.concatenate([total, jnp.zeros((4, 128), F32)], axis=0).astype(BF)
    for n in range(16):
        out[n] = piece


def line_kernel(pieces, out):
    both = [jnp.concatenate([pieces[zl].astype(F32), pieces[8 + zl].astype(F32)], axis=0) for zl in range(8)]
    pad = jnp.zeros((48, 16), F32)
    groups = [jnp.concatenate([b[:, 30 * a : 30 * a + 30] for b in both] + [pad], axis=1) for a in range(4)]
    block = jnp.concatenate(groups, axis=1).astype(BF)
    for n in range(16):
        out[n] = block


def pair(v):
    return v[:, :64] + v[:, 64:]


def moments(chunks):
    s = q = 0.0
    for v in chunks:
        v = v.reshape(-1, 8, v.shape[1])
        s, q = s + jnp.sum(v, axis=0), q + jnp.sum(v * v, axis=0)
    return s, q


def act_kernel(video, gain, shift, same, perm_hbm, out_hbm, perm, out, sems):
    move = Mover(sems)
    perm_copy = move.start(perm_hbm, perm)
    chunk = 256
    column = lax.rem(lax.broadcasted_iota(jnp.int32, (chunk, 256), 0), COLS)
    low = lax.broadcasted_iota(jnp.int32, (chunk, 128), 1) < 64

    def shifted(v):
        edge = column[:, : v.shape[1]]
        before = jnp.where(edge == 0, 0.0, pltpu.roll(v, 1, 0))
        after = jnp.where(edge == COLS - 1, 0.0, pltpu.roll(v, chunk - 1, 0))
        return before, v, after

    main = lambda i: video[pl.ds(i * chunk, chunk), 0:256].astype(F32)
    tail = lambda i: video[pl.ds(i * chunk, chunk), 256:320].astype(F32)
    rest = lambda i: jnp.concatenate([tail(i), tail(i + 3)], axis=1)
    s, q = moments(main(i) for i in range(6))
    s2, q2 = moments(rest(i) for i in range(3))
    s = jnp.concatenate([s, pair(s2)], axis=1)
    q = jnp.concatenate([q, pair(q2)], axis=1)
    both = exact(jnp.concatenate([s, q], axis=0), same[...]) / (CELLS * C // GROUPS)
    mean = jnp.sum(both[:8], axis=0, keepdims=True)
    square = jnp.sum(both[8:], axis=0, keepdims=True)
    scale = lax.rsqrt(square - mean * mean + EPS) * gain[...].reshape(1, C)
    offset = shift[...].reshape(1, C) - mean * scale
    scale2 = jnp.concatenate([scale[:, 256:], scale[:, 256:]], axis=1)
    offset2 = jnp.concatenate([offset[:, 256:], offset[:, 256:]], axis=1)
    scale, offset = scale[:, :256], offset[:, :256]
    out[pl.ds(0, COLS), :] = jnp.zeros((COLS, KPAD), BF)
    out[pl.ds(CELLS + COLS, COLS), :] = jnp.zeros((COLS, KPAD), BF)
    perm_copy.wait()
    swap = lambda v: pltpu.roll(v, 64, 1)
    for i in range(3):
        before2, v2, after2 = shifted(silu(rest(i) * scale2 + offset2).astype(BF).astype(F32))
        tails = [
            (jnp.where(low, before2, swap(v2)), jnp.where(low, after2, 0.0)),
            (jnp.where(low, swap(before2), v2), jnp.where(low, swap(after2), 0.0)),
        ]
        for n in range(2):
            at = i + 3 * n
            taps = shifted(silu(main(at) * scale + offset).astype(BF).astype(F32))
            taps = jnp.concatenate(taps + tails[n], axis=1).astype(BF)
            total = jnp.dot(taps, perm[...], preferred_element_type=F32)
            out[pl.ds(at * chunk + COLS, chunk), :] = total.astype(BF)
    move.start(out, out_hbm).wait()


def place_weights(half, block, w):
    for y in range(4):
        for x in range(4):
            for a in range(4):
                rows = pl.ds(pl.multiple_of(half + 48 * y, 16), 48)
                w[a, rows, 256 * x : 256 * x + 256] = block[4 * y + x, :, 256 * a : 256 * a + 256]


def own_kernel(cols_hbm, own_hbm, other_hbm, emb, order, first_hbm, second_hbm, stats, last_hbm, cols, own, other, hidden, w, natural, sems):
    move = Mover(sems)
    own_copy = move.start(own_hbm, own)
    other_copy = move.start(other_hbm, other)
    cols_copy = move.start(cols_hbm, cols)
    mine = lax.axis_index("core") * HALF
    own_copy.wait()
    place_weights(mine, own, w)
    other_copy.wait()
    place_weights(HALF - mine, other, w)
    cols_copy.wait()
    for a in range(4):
        natural[a] = jnp.dot(order[...], w[a], preferred_element_type=F32).astype(BF)
    s = q = jnp.zeros((8, C), F32)
    for i in (0, 3, 1, 4, 2, 5):
        total = jnp.zeros((C, 256), F32)
        for a in range(3):
            total += nt(natural[a], cols[pl.ds(i * 256 + COLS * a, 256), :])
        h = (total.T + emb[0]).astype(BF)
        hidden[pl.ds(i * 256, 256), :] = h[:, :128]
        hidden[pl.ds(CELLS + i * 256, 256), :] = h[:, 128:256]
        h = h.astype(F32)
        if i < 3:
            rest = h[:, 256:]
        else:
            both = jnp.concatenate([rest, h[:, 256:]], axis=1)
            hidden[pl.ds(2 * CELLS + (i - 3) * 256, 256), :] = both.astype(BF)
        h = h.reshape(32, 8, C)
        s, q = s + jnp.sum(h, axis=0), q + jnp.sum(h * h, axis=0)
    copies = [move.start(hidden.at[pl.ds(0, FIRST)], first_hbm), move.start(hidden.at[pl.ds(FIRST, PACKED - FIRST)], second_hbm)]
    copies.append(move.start(natural.at[3], last_hbm))
    s = jnp.sum(s, axis=0, keepdims=True)
    q = jnp.sum(q, axis=0, keepdims=True)
    tail = jnp.concatenate([s[:, 256:], q[:, 256:]], axis=1)
    rows = [s[:, :128], s[:, 128:256], q[:, :128], q[:, 128:256], tail, jnp.zeros((3, 128), F32)]
    block = jnp.concatenate(rows, axis=0)
    for n in range(32):
        stats[n] = block
    for copy in copies:
        copy.wait()


def temporal_kernel(w, perm, out):
    frame = lax.axis_index("zl") * 4 + lax.axis_index("x")
    lane = lax.broadcasted_iota(jnp.int32, (1, KPAD), 1)
    tap = jnp.where(lane < 768, lane // 256, (lane - 768) // 64)
    keep = jnp.where(tap == 0, (frame > 0).astype(F32), jnp.where(tap == 2, (frame < 31).astype(F32), 1.0))
    out[...] = (jnp.dot(w[...], perm[...], preferred_element_type=F32) * keep).astype(BF)


def final_kernel(first0, second0, first1, second1, first2, second2, stats, gain, shift, same, bias, last, out):
    def rows(frame, start):
        first, second = frame
        ref, at = (first, start) if start < FIRST else (second, start - FIRST)
        return ref[pl.ds(at, 256), :].astype(F32)

    total = stats[0]
    for n in range(1, 32):
        total = total + stats[n]
    s = jnp.concatenate([total[0:1], total[1:2], total[4:5, :64]], axis=1)
    q = jnp.concatenate([total[2:3], total[3:4], total[4:5, 64:]], axis=1)
    both = jnp.concatenate([s, q, jnp.zeros((6, C), F32)], axis=0)
    both = exact(both, same[...]) / (CELLS * 32 * C // GROUPS)
    mean, square = both[0:1], both[1:2]
    scale = lax.rsqrt(square - mean * mean + EPS) * gain[...].reshape(1, C)
    offset = shift[...].reshape(1, C) - mean * scale
    tiles = [(scale[:, n : n + 128], offset[:, n : n + 128]) for n in (0, 128)]
    tiles.append(tuple(jnp.concatenate([v[:, 256:], v[:, 256:]], axis=1) for v in (scale, offset)))
    bias_row = bias[...].reshape(1, C)
    low = lax.broadcasted_iota(jnp.int32, (256, 128), 1) < 64
    swap = lambda v: pltpu.roll(v, 64, 1)
    frames = ((first0, second0), (first1, second1), (first2, second2))

    def mix(h, start, tile):
        v = rows(h, start)
        return silu(v * tiles[tile][0] + tiles[tile][1])

    for i in range(3):
        a, b, c = (mix(h, 2 * CELLS + i * 256, 2) for h in frames)
        tails = [
            (jnp.where(low, a, swap(b)), jnp.where(low, c, 0.0)),
            (jnp.where(low, swap(a), b), jnp.where(low, swap(c), 0.0)),
        ]
        rest = rows(frames[1], 2 * CELLS + i * 256)
        for n in range(2):
            at = i + 3 * n
            parts = [mix(h, tile * CELLS + at * 256, tile) for h in frames for tile in range(2)]
            taps = jnp.concatenate(parts + list(tails[n]), axis=1).astype(BF)
            moved = (nt(last[...], taps).T + bias_row).astype(BF).astype(F32)
            here = pl.ds(at * 256, 256)
            h = [rows(frames[1], tile * CELLS + at * 256) for tile in range(2)]
            h.append(rest[:, :64] if n == 0 else rest[:, 64:])
            out[here, :] = (moved + jnp.concatenate(h, axis=1)).astype(BF)


FILL = 5_000_000_000
FRAME = ("zl", "x")
FORWARD = [(i, i + 1) for i in range(31)]
BACKWARD = [(i + 1, i) for i in range(31)]


def body(video, emb, gain1, shift1, gain2, shift2, sw, tw, bias):
    struct = jax.ShapeDtypeStruct
    const = lambda a, t=BF: jnp.asarray(a, t)
    sems = pltpu.SemaphoreType.DMA
    buffer = lambda *shape: pltpu.VMEM(shape, BF)
    cols = (CELLS + 2 * COLS, KPAD)
    blocks = (16, 48, KPAD)

    (pieces,) = call(pack_kernel, [struct((16, 24, 128), BF)], "vv")(sw.transpose(0, 2, 1), tw.transpose(1, 0, 2))
    line = lax.all_to_all(pieces, ("zh", "zl"), 0, 0)
    (block,) = call(line_kernel, [struct(blocks, BF)], "v")(line)
    own = lax.all_to_all(block, ("y", "x"), 0, 0)
    (cols1,) = call(
        act_kernel,
        [struct(cols, BF)],
        "vvvva",
        "a",
        [buffer(KPAD, KPAD), buffer(*cols), sems((2,))],
        FILL,
    )(video.reshape(CELLS, C), gain1, shift1, const(SAME1, F32), const(ACT_PERM))
    own, cols1 = lax.optimization_barrier((own, cols1))
    other = lax.ppermute(own, "core", [(0, 1), (1, 0)])

    first1, second1, stats, w = call(
        own_kernel,
        [
            struct((FIRST, 128), BF),
            struct((PACKED - FIRST, 128), BF),
            struct((32, 8, 128), F32),
            struct((C, KPAD), BF),
        ],
        "aaavv",
        "aava",
        [
            buffer(*cols),
            buffer(*blocks),
            buffer(*blocks),
            buffer(PACKED, 128),
            buffer(4, CPAD, KPAD),
            buffer(4, C, KPAD),
            sems((6,)),
        ],
    )(cols1, own, other, emb, const(ORDER))
    first0 = lax.ppermute(first1, FRAME, FORWARD)
    first2 = lax.ppermute(first1, FRAME, BACKWARD)
    stats = lax.all_to_all(stats, FRAME, 0, 0)
    second0 = lax.ppermute(second1, FRAME, FORWARD)
    second2 = lax.ppermute(second1, FRAME, BACKWARD)
    (last,) = call(temporal_kernel, [struct((C, KPAD), BF)], "vv", flops=5_000_000_000)(w, const(TEMP_PERM))
    (out,) = call(final_kernel, [struct((CELLS, C), BF)], "v" * 12)(
        first0, second0, first1, second1, first2, second2, stats, gain2, shift2, const(SAME1, F32), bias, last
    )
    return out.reshape(video.shape)


def solution(mesh):
    split = Mesh(mesh.devices.reshape(4, 2, 2, 8, 4), ("y", "zh", "core", "zl", "x"))
    dp = ("y", "zh", "core")
    data = P(dp, FRAME, None, None, None)
    placed = (data, P(dp, FRAME, None), P(), P(), P(), P(), P(None, FRAME, dp), P(None, FRAME, dp), P())
    return jax.shard_map(body, mesh=split, in_specs=placed, out_specs=data, check_vma=False)
```
